128 devices in a mesh: gx: 16 (over z, y_lo, core), gy: 8 (over x, y_hi).
Axes of the slice: x: 4, y: 4 (y_hi: 2, y_lo: 2; y = y_hi * 2 + y_lo), z: 4, core: 2. Of those that a mesh axis runs over, the one named last changes fastest.
Arguments:
- raw_stack: float32 [2, 128, 256, 2048], P(None, ('gx', 'gy')), may hold values from 0 to 8
- psf_taps: float32 [3, 2, 31], replicated, may hold values from 0.05 to 1
Outputs:
- estimate: float32 [2, 128, 256, 2048], P(None, None, 'gy', 'gx')
The draws below stay inside these ranges and needn't reach their ends.
All inputs are finite; a program needn't handle non-finite values.
Results may differ from the reference program's by a relative error of at most 0.0001.
Values sent between devices are 32-bit elements; how exact they have to be, the bound alone decides.
No kernel may reach another device: no remote copies, remote signals or barrier semaphores. Data moves between devices by JAX's collectives and lax.ppermute only.
A program may use at most 192 MiB of HBM per device.

```python
import math
import jax
import jax.numpy as jnp
from jax import lax

CH = 2
NY = 2048
TAPS = 31
ITERS = 2
NX = 256
Z = 128


def draw_raw_stack(key, part):
    key_level = jax.random.fold_in(key, 11)
    key_stripe = jax.random.fold_in(key, 12)
    base_level = jax.random.uniform(key_level, (CH, Z, NX, NY), jnp.float32, 0.25, 4.0)
    stripe_gain = jnp.exp(jax.random.uniform(key_stripe, (CH, Z, 1, NY), jnp.float32, math.log(0.5), math.log(2.0)))
    return base_level * stripe_gain


def setup_inputs(seed: int = 0) -> dict:
    keys = jax.random.split(jax.random.key(seed), 3)
    return {
        "raw_stack": draw_raw_stack(jax.random.fold_in(keys[2], 71), 0),
        "psf_taps": jnp.clip(jnp.exp(jax.random.uniform(keys[1], (3, CH, TAPS), jnp.float32, math.log(0.05), math.log(1.0))), 0.05, 1.0),
    }


BACKGROUND = 0.5
SIGMA_ACROSS = 48.0
SIGMA_ALONG = 96.0


def smoothing_table(length_cells, spread_cells, circular):
    places = lax.iota(jnp.int32, length_cells)
    offset = jnp.abs(places[:, None] - places[None, :])
    if circular:
        offset = jnp.minimum(offset, length_cells - offset)
    scaled = offset.astype(jnp.float32) / spread_cells
    kernel_table = jnp.exp(-0.5 * scaled * scaled)
    return kernel_table / jnp.sum(kernel_table, axis=1, keepdims=True)


def filter_axis(volume, kernel_taps, axis_index):
    half_taps = kernel_taps.shape[1] // 2
    results = []
    for channel in range(volume.shape[0]):
        shifted_axes = jnp.moveaxis(volume[channel], axis_index - 1, -1)
        line_rows = shifted_axes.reshape(-1, 1, shifted_axes.shape[-1])
        kernel = kernel_taps[channel].reshape(1, 1, -1)
        output = lax.conv_general_dilated(line_rows, kernel, (1,), [(half_taps, half_taps)], precision=lax.Precision.HIGHEST)
        results.append(jnp.moveaxis(output.reshape(shifted_axes.shape), -1, axis_index - 1))
    return jnp.stack(results)


def blur_volume(volume, kernel_set):
    result = filter_axis(volume, kernel_set[0], 1)
    result = filter_axis(result, kernel_set[1], 2)
    return filter_axis(result, kernel_set[2], 3)


def reference(raw_stack, psf_taps):
    across_table = smoothing_table(NX, SIGMA_ACROSS, False)
    along_table = smoothing_table(NY, SIGMA_ALONG, True)

    def destripe(plane):
        smoothed = jnp.einsum('ij,cjy->ciy', across_table, plane, precision=lax.Precision.HIGHEST)
        stripes = smoothed - jnp.einsum('cxj,jy->cxy', smoothed, along_table, precision=lax.Precision.HIGHEST)
        return jnp.maximum(plane - stripes, 0.0)

    cleaned = jnp.moveaxis(lax.map(destripe, jnp.moveaxis(raw_stack, 1, 0)), 0, 1)
    forward = psf_taps / jnp.sum(psf_taps, axis=2, keepdims=True)
    backward = forward[:, :, ::-1]
    estimate = cleaned
    for iteration in range(ITERS):
        blurred = blur_volume(estimate, forward)
        ratio_field = cleaned / (blurred + BACKGROUND)
        estimate = estimate * blur_volume(ratio_field, backward)
    return estimate
```

```python
import functools

import jax
import jax.numpy as jnp
import numpy as np
from jax import lax
from jax.experimental import pallas as pl
from jax.experimental.pallas import tpu as pltpu
from jax.sharding import PartitionSpec as P

CH, NZ, NX, NY = 2, 128, 256, 2048
TAPS, HALF = 31, 15
ITERS = 2
BACKGROUND = 0.5
SIGMA_ACROSS = 48.0
SIGMA_ALONG = 96.0

LINES = 32
BLOCKS = NY // LINES
AXES = ("gx", "gy")
F32, BF16 = jnp.float32, jnp.bfloat16
VMEM_LIMIT = 60 * 1024 * 1024


def rank(x, yh, yl, z, core):
    return ((z * 2 + yl) * 2 + core) * 8 + x * 2 + yh


def place(block):
    core, row, step = block & 1, block >> 3, (block >> 1) & 3
    z, k = row >> 1, row & 1
    return (step if k == 0 else 3 - step), k ^ (z & 1), z, core


def device_of(channel, block):
    x, yl, z, core = place(block)
    return rank(x, channel, yl, z, core)


UP = [(device_of(c, b), device_of(c, (b + 1) % BLOCKS)) for c in range(CH) for b in range(BLOCKS)]
DOWN = [(target, source) for source, target in UP]

ROUNDS = 8


def final_target(channel, block, j):
    x, _, _, core = place(block)
    xd = (x + 2 * core + (j >> 1)) % 4
    x8 = 2 * xd + (channel ^ (j & 1) ^ core)
    return x8, (block >> 2) * 8 + x8


FINAL = [
    [(device_of(c, b), final_target(c, b, j)[1]) for c in range(CH) for b in range(BLOCKS)]
    for j in range(ROUNDS)
]


def meta_table():
    meta = np.zeros((128, 2 + 2 * ROUNDS), np.int32)
    for c in range(CH):
        for b in range(BLOCKS):
            me = device_of(c, b)
            meta[me, 0] = b > 0
            meta[me, 1] = b < BLOCKS - 1
            for j in range(ROUNDS):
                x8, target = final_target(c, b, j)
                meta[me, 2 + j] = x8
                meta[target, 2 + ROUNDS + j] = c * 4 + (b & 3)
    return meta


def np_split(table):
    high = table.astype(np.float32).astype(jnp.bfloat16)
    low = (table - high.astype(np.float64)).astype(np.float32).astype(jnp.bfloat16)
    return high, low


def destripe_tables():
    i = np.arange(NX, dtype=np.float64)
    across = np.exp(-0.5 * ((i[:, None] - i[None, :]) / SIGMA_ACROSS) ** 2)
    across = across / across.sum(axis=1, keepdims=True)
    n = np.arange(NY, dtype=np.float64)
    c = np.minimum(n, NY - n)
    ring = np.exp(-0.5 * (c / SIGMA_ALONG) ** 2)
    ring = ring / ring.sum()
    along = ring[(np.arange(NY)[:, None] - np.arange(NY)[None, :]) % NY]
    h, q = NY // 2, NY // 4
    even = along[:h, :h] + along[:h, h:]
    odd = along[:h, :h] - along[:h, h:]
    even_even = even[:q, :q] + even[:q, q:]
    even_odd = even[:q, :q] - even[:q, q:]
    out = []
    for table in (across.T, odd, even_even, even_odd):
        out.extend(np_split(table))
    return out


def split(v):
    high = v.astype(BF16)
    return high, (v - high.astype(F32)).astype(BF16)


def dot(a, b):
    return jnp.dot(a, b, preferred_element_type=F32)


def dot3(a_high, a_low, b_high, b_low):
    return dot(a_high, b_high) + (dot(a_high, b_low) + dot(a_low, b_high))


def destripe_kernel(raw, ah, al, oh, ol, eeh, eel, eoh, eol, out, rt, sm, dh, dl, s1h, s1l, d1h, d1l):
    h, q = NY // 2, NY // 4

    @pl.loop(0, NY // 256)
    def _(i):
        r = pl.multiple_of(i * 256, 256)
        tile = raw[0, 0, :, pl.ds(r, 256)].T
        rt[pl.ds(r, 256), :] = tile
        th, tl = split(tile)
        sm[pl.ds(r, 256), :] = dot3(th, tl, ah[...], al[...])

    @pl.loop(0, q // 128)
    def _(i):
        r = pl.multiple_of(i * 128, 128)
        parts = [sm[pl.ds(r + m * q, 128), :] for m in range(4)]
        for m in range(2):
            hi, lo = split(0.5 * (parts[m] - parts[m + 2]))
            dh[pl.ds(r + m * q, 128), :] = hi
            dl[pl.ds(r + m * q, 128), :] = lo
        top = 0.5 * (parts[0] + parts[2])
        bottom = 0.5 * (parts[1] + parts[3])
        hi, lo = split(0.5 * (top + bottom))
        s1h[pl.ds(r, 128), :] = hi
        s1l[pl.ds(r, 128), :] = lo
        hi, lo = split(0.5 * (top - bottom))
        d1h[pl.ds(r, 128), :] = hi
        d1l[pl.ds(r, 128), :] = lo

    def emit(row, smooth):
        for m in range(8):
            x, yl, z, core = place(row // LINES + m)
            at = pl.ds(row + m * LINES, LINES)
            part = smooth[m * LINES : (m + 1) * LINES, :]
            clean = jnp.maximum(rt[at, :] - (sm[at, :] - part), 0.0)
            gx = (z * 2 + yl) * 2 + core
            out[gx, x, 0, 0:LINES, :] = clean[:, :128]
            out[gx, x, 0, LINES : 2 * LINES, :] = clean[:, 128:]

    for i in range(2):
        at = slice(i * 256, (i + 1) * 256)
        ee = dot3(eeh[at, :], eel[at, :], s1h[...], s1l[...])
        eo = dot3(eoh[at, :], eol[at, :], d1h[...], d1l[...])
        for m in range(2):
            row = m * q + i * 256
            even = ee + eo if m == 0 else ee - eo
            rows = slice(row, row + 256)
            odd = dot3(oh[rows, :], ol[rows, :], dh[...], dl[...])
            emit(row, even + odd)
            emit(h + row, even - odd)


def destripe(raw_stack):
    tables = [jnp.asarray(t) for t in destripe_tables()]
    whole = pl.BlockSpec(memory_space=pltpu.VMEM)
    return pl.pallas_call(
        destripe_kernel,
        grid=(CH,),
        in_specs=[pl.BlockSpec((1, 1, NX, NY), lambda c: (c, 0, 0, 0))] + [whole] * 8,
        out_specs=pl.BlockSpec((16, 4, 1, 64, 128), lambda c: (0, 0, c, 0, 0)),
        out_shape=jax.ShapeDtypeStruct((16, 4, CH, 64, 128), F32),
        scratch_shapes=[
            pltpu.VMEM((NY, NX), F32),
            pltpu.VMEM((NY, NX), F32),
            pltpu.VMEM((NY // 2, NX), BF16),
            pltpu.VMEM((NY // 2, NX), BF16),
        ]
        + [pltpu.VMEM((NY // 4, NX), BF16)] * 4,
        compiler_params=pltpu.CompilerParams(vmem_limit_bytes=VMEM_LIMIT),
        name="destripe",
    )(raw_stack, *tables)


def band(weights, size):
    shape = (size, size)
    lag = lax.broadcasted_iota(jnp.int32, shape, 1) - lax.broadcasted_iota(jnp.int32, shape, 0)
    out = jnp.zeros(shape, F32)
    for k in range(TAPS):
        out = jnp.where(lag == k - HALF, weights[k], out)
    return out


def tables_kernel(taps, *outs):
    for way in range(2):
        z_table, xh, xl = outs[3 * way : 3 * way + 3]
        hi, lo = split(band(tap_list(taps, 0, 1 - way), NZ))
        for half in range(2):
            rows = slice(half * NZ, (half + 1) * NZ)
            z_table[rows, :NZ] = hi
            z_table[rows, NZ:] = lo
        hi, lo = split(band(tap_list(taps, 1, way), NX))
        xh[...] = hi
        xl[...] = lo


def filter_tables(taps):
    square = jax.ShapeDtypeStruct((256, 256), BF16)
    outs = pl.pallas_call(
        tables_kernel,
        in_specs=[pl.BlockSpec(memory_space=pltpu.SMEM)],
        out_shape=[square] * 6,
        compiler_params=pltpu.CompilerParams(vmem_limit_bytes=VMEM_LIMIT),
        cost_estimate=pl.CostEstimate(flops=10**10, bytes_accessed=10**6, transcendentals=0),
        name="tables",
    )(taps)
    return outs[:3], outs[3:]


def tap_list(taps, axis, way):
    return [taps[axis, k if way == 0 else TAPS - 1 - k] for k in range(TAPS)]


def filter_z(v, z_table):
    hi, lo = split(v)
    both = dot(jnp.concatenate([hi, lo], axis=1), z_table)
    return both[:, :NZ] + both[:, NZ:]


def filter_x_pair(hi, lo, xh, xl):
    return dot(xh, hi) + (dot(xh, lo) + dot(xl, hi))


EDGE_SHAPES = ((HALF, NX, NZ), (LINES - 2 * HALF, NX, NZ), (HALF, NX, NZ))


def for_pairs(pair, low, mid, high):
    @pl.loop(0, HALF // 2)
    def _(i):
        a, b = pair(2 * i)
        low[2 * i] = a
        low[2 * i + 1] = b

    a, b = pair(HALF - 1)
    low[HALF - 1] = a
    mid[0] = b
    a, b = pair(HALF + 1)
    mid[1] = a
    high[0] = b

    @pl.loop(0, HALF // 2)
    def _(i):
        a, b = pair(HALF + 3 + 2 * i)
        high[1 + 2 * i] = a
        high[2 + 2 * i] = b


def arrive_kernel(got, z_table, xh, xl, cleaned, low, mid, high):
    def pair(y):
        his, los = [], []
        for m in range(2):
            for half in range(2):
                tile = got[pl.ds(half * LINES + y + m, NZ, stride=2 * LINES), :].T
                cleaned[y + m, half * 128 : (half + 1) * 128, :] = tile
            hi, lo = split(filter_z(cleaned[y + m], z_table[...]))
            his.append(hi)
            los.append(lo)
        both = filter_x_pair(
            jnp.concatenate(his, axis=1), jnp.concatenate(los, axis=1), xh[...], xl[...]
        )
        return both[:, :NZ], both[:, NZ:]

    for_pairs(pair, low, mid, high)


def arrive(got, tables):
    whole = pl.BlockSpec(memory_space=pltpu.VMEM)
    return pl.pallas_call(
        arrive_kernel,
        in_specs=[whole] * 4,
        out_specs=[whole] * 4,
        out_shape=[jax.ShapeDtypeStruct((LINES, NX, NZ), F32)]
        + [jax.ShapeDtypeStruct(s, F32) for s in EDGE_SHAPES],
        compiler_params=pltpu.CompilerParams(vmem_limit_bytes=VMEM_LIMIT),
        name="arrive",
    )(got, *tables)


XB = 64


def own_kernel(way, taps, low, mid, high, out):
    weights = [jnp.full((8, NZ), tap, F32) for tap in tap_list(taps, 2, way)]

    def line(j, at):
        if j < HALF:
            return low[j, at, :]
        if j < LINES - HALF:
            return mid[j - HALF, at, :]
        return high[j - (LINES - HALF), at, :]

    @pl.loop(0, XB // 8)
    def _(t):
        at = pl.ds(pl.multiple_of(t * 8, 8), 8)
        for first in range(0, LINES, 8):
            sums = [None] * 8
            for j in range(max(0, first - HALF), min(LINES, first + 8 + HALF)):
                v = line(j, at)
                for m in range(8):
                    k = j - (first + m) + HALF
                    if 0 <= k < TAPS:
                        term = weights[k] * v
                        sums[m] = term if sums[m] is None else sums[m] + term
            for m in range(8):
                out[first + m, at, :] = sums[m]


def own_lines(way, taps, low, mid, high):
    return pl.pallas_call(
        functools.partial(own_kernel, way),
        grid=(NX // XB,),
        in_specs=[pl.BlockSpec(memory_space=pltpu.SMEM)]
        + [pl.BlockSpec((s[0], XB, NZ), lambda i: (0, i, 0)) for s in EDGE_SHAPES],
        out_specs=pl.BlockSpec((LINES, XB, NZ), lambda i: (0, i, 0)),
        out_shape=jax.ShapeDtypeStruct((LINES, NX, NZ), F32),
        compiler_params=pltpu.CompilerParams(vmem_limit_bytes=VMEM_LIMIT),
        cost_estimate=pl.CostEstimate(
            flops=2 * 31 * LINES * NX * NZ * 100, bytes_accessed=2 * LINES * NX * NZ * 4, transcendentals=0
        ),
        name="own_lines",
    )(taps, low, mid, high)


def add_halo(way, taps, meta, partial, below, above, at, use):
    weights = [jnp.full((8, NZ), tap, F32) for tap in tap_list(taps, 2, way)]
    has_below, has_above = meta[0] != 0, meta[1] != 0
    for first in range(0, LINES, 8):
        sums = [partial[first + m, at, :] for m in range(8)]
        for j in range(HALF):
            if j >= first:
                v = jnp.where(has_below, below[j, at, :], 0.0)
                for m in range(8):
                    k = j - (first + m)
                    if 0 <= k < HALF:
                        sums[m] = sums[m] + weights[k] * v
        for j in range(HALF):
            if LINES + j - (first + 7) <= HALF:
                v = jnp.where(has_above, above[j, at, :], 0.0)
                for m in range(8):
                    k = LINES + j - (first + m) + HALF
                    if k < TAPS:
                        sums[m] = sums[m] + weights[k] * v
        for m in range(8):
            use(first + m, sums[m])


def step_kernel(ratio, taps, meta, partial, below, above, other, z_table, xh, xl, *rest):
    if ratio:
        low, mid, high, work, zhi, zlo = rest
    else:
        work, low, mid, high, zhi, zlo = rest
    i = pl.program_id(0)

    @pl.loop(0, XB // 8)
    def _(t):
        at = pl.ds(pl.multiple_of(t * 8, 8), 8)

        def use(y, total):
            if ratio:
                work[y, at, :] = other[y, at, :] / (total + BACKGROUND)
            else:
                work[y, at, :] = other[y, at, :] * total

        add_halo(0 if ratio else 1, taps, meta, partial, below, above, at, use)

    to = pl.ds(pl.multiple_of(i * XB, XB), XB)

    @pl.loop(0, LINES // 4)
    def _(g):
        v = work[pl.ds(g * 4, 4)].reshape(4 * XB, NZ)
        hi, lo = split(filter_z(v, z_table[...]))
        zhi[pl.ds(g * 4, 4), to, :] = hi.reshape(4, XB, NZ)
        zlo[pl.ds(g * 4, 4), to, :] = lo.reshape(4, XB, NZ)

    @pl.when(i == NX // XB - 1)
    def _():
        def pair(y):
            hi = jnp.concatenate([zhi[y], zhi[y + 1]], axis=1)
            lo = jnp.concatenate([zlo[y], zlo[y + 1]], axis=1)
            both = filter_x_pair(hi, lo, xh[...], xl[...])
            return both[:, :NZ], both[:, NZ:]

        for_pairs(pair, low, mid, high)


def step(ratio, taps, meta, partial, below, above, other, tables):
    smem = pl.BlockSpec(memory_space=pltpu.SMEM)
    whole = pl.BlockSpec(memory_space=pltpu.VMEM)
    lines = pl.BlockSpec((LINES, XB, NZ), lambda i: (0, i, 0))
    edge = pl.BlockSpec((HALF, XB, NZ), lambda i: (0, i, 0))
    full = jax.ShapeDtypeStruct((LINES, NX, NZ), F32)
    edges = [jax.ShapeDtypeStruct(s, F32) for s in EDGE_SHAPES]
    scratch = [pltpu.VMEM((LINES, NX, NZ), BF16)] * 2
    return pl.pallas_call(
        functools.partial(step_kernel, ratio),
        grid=(NX // XB,),
        in_specs=[smem, smem, lines, edge, edge, lines] + [whole] * 3,
        out_specs=([] if ratio else [lines]) + [whole] * 3,
        out_shape=([] if ratio else [full]) + edges,
        scratch_shapes=([pltpu.VMEM((LINES, XB, NZ), F32)] if ratio else []) + scratch,
        compiler_params=pltpu.CompilerParams(vmem_limit_bytes=VMEM_LIMIT),
        name="ratio_step" if ratio else "estimate_step",
    )(taps, meta, partial, below, above, other, *tables)


def last_kernel(meta, taps, partial, below, above, other, out):
    @pl.loop(0, LINES // 8)
    def _(t):
        at = pl.ds(pl.multiple_of(t * 8, 8), 8)

        def use(y, total):
            out[0, y, at, :] = other[y, at, :] * total

        add_halo(1, taps, meta, partial, below, above, at, use)


def last(taps, meta, partial, below, above, other, first, count):
    smem = pl.BlockSpec(memory_space=pltpu.SMEM)

    def at(i, meta):
        return (0, meta[2 + first + i], 0)

    lines = pl.BlockSpec((LINES, 32, NZ), at)
    edge = pl.BlockSpec((HALF, 32, NZ), at)
    return pl.pallas_call(
        last_kernel,
        grid_spec=pltpu.PrefetchScalarGridSpec(
            num_scalar_prefetch=1,
            grid=(count,),
            in_specs=[smem, lines, edge, edge, lines],
            out_specs=pl.BlockSpec((1, LINES, 32, NZ), lambda i, *_: (i, 0, 0, 0)),
        ),
        out_shape=jax.ShapeDtypeStruct((count, LINES, 32, NZ), F32),
        compiler_params=pltpu.CompilerParams(vmem_limit_bytes=VMEM_LIMIT),
        name="last_step",
    )(meta, taps, partial, below, above, other)


def leave_kernel(meta, *refs):
    parts, out, held = refs[:ROUNDS], refs[ROUNDS], refs[ROUNDS + 1]
    rows = LINES * 32
    for j in range(ROUNDS):
        base = meta[2 + ROUNDS + j] * rows

        @pl.loop(0, LINES)
        def _(y):
            held[pl.ds(pl.multiple_of(base + y * 32, 32), 32), :] = parts[j][0, y]

    @pl.loop(0, CH * 32)
    def _(i):
        start = (i // 32) * (128 * 32) + lax.rem(i, 32)
        tile = held[pl.ds(start, 128, stride=32), :].T
        out[pl.ds(start, 128, stride=32), :] = tile


def leave(meta, parts):
    whole = pl.BlockSpec(memory_space=pltpu.VMEM)
    return pl.pallas_call(
        leave_kernel,
        in_specs=[pl.BlockSpec(memory_space=pltpu.SMEM)] + [whole] * ROUNDS,
        out_specs=whole,
        out_shape=jax.ShapeDtypeStruct((CH * NZ * 32, 128), F32),
        scratch_shapes=[pltpu.VMEM((CH * 128 * 32, NZ), F32)],
        compiler_params=pltpu.CompilerParams(vmem_limit_bytes=VMEM_LIMIT),
        name="leave",
    )(meta, *parts)


def local(raw_stack, psf_taps):
    me = lax.axis_index("gx") * 8 + lax.axis_index("gy")
    channel = lax.rem(lax.axis_index("gy"), 2)
    meta = lax.dynamic_index_in_dim(jnp.asarray(meta_table()), me, keepdims=False)
    taps = lax.dynamic_index_in_dim(psf_taps, channel, axis=1, keepdims=False)
    taps = taps / jnp.sum(taps, axis=1, keepdims=True)

    blocks = destripe(raw_stack).reshape(128, 64, 128)
    got = lax.all_to_all(blocks, AXES, split_axis=0, concat_axis=0, tiled=True)
    tables = filter_tables(taps)
    cleaned, low, mid, high = arrive(got.reshape(128 * 64, 128), tables[0])

    estimate = cleaned
    for blur in range(2 * ITERS):
        way = blur % 2
        below = lax.ppermute(high, AXES, UP)
        above = lax.ppermute(low, AXES, DOWN)
        partial = own_lines(way, taps, low, mid, high)
        if blur == 2 * ITERS - 1:
            parts = [last(taps, meta, partial, below, above, estimate, j, 1) for j in range(ROUNDS)]
        elif way == 0:
            low, mid, high = step(True, taps, meta, partial, below, above, cleaned, tables[1])
        else:
            estimate, low, mid, high = step(
                False, taps, meta, partial, below, above, estimate, tables[0]
            )
    parts = [lax.ppermute(part, AXES, FINAL[j]) for j, part in enumerate(parts)]
    return leave(meta, parts).reshape(CH, NZ, 32, 128)


def solution(mesh):
    in_specs = (P(None, AXES, None, None), P())
    out_specs = P(None, None, "gy", "gx")
    return jax.shard_map(local, mesh=mesh, in_specs=in_specs, out_specs=out_specs, check_vma=False)
```

```python
import functools

import jax
import jax.numpy as jnp
import numpy as np
from jax import lax
from jax.experimental import pallas as pl
from jax.experimental.pallas import tpu as pltpu
from jax.sharding import PartitionSpec as P

CH, NZ, NX, NY = 2, 128, 256, 2048
TAPS, HALF = 31, 15
ITERS = 2
BACKGROUND = 0.5
SIGMA_ACROSS = 48.0
SIGMA_ALONG = 96.0

LINES = 32
BLOCKS = NY // LINES
AXES = ("gx", "gy")
F32, BF16 = jnp.float32, jnp.bfloat16
VMEM_LIMIT = 24 * 1024 * 1024
HL = LINES // 2


def rank(x, yh, yl, z, core):
    return ((z * 2 + yl) * 2 + core) * 8 + x * 2 + yh


def place(block):
    core, row, step = block & 1, block >> 3, (block >> 1) & 3
    z, k = row >> 1, row & 1
    return (step if k == 0 else 3 - step), k ^ (z & 1), z, core


def device_of(channel, block):
    x, yl, z, core = place(block)
    return rank(x, channel, yl, z, core)


UP = [(device_of(c, b), device_of(c, (b + 1) % BLOCKS)) for c in range(CH) for b in range(BLOCKS)]
DOWN = [(target, source) for source, target in UP]

ROUNDS = 8


def final_target(channel, block, j):
    x, _, _, core = place(block)
    xd = (x + 2 * core + (j >> 1)) % 4
    x8 = 2 * xd + (channel ^ (j & 1) ^ core)
    return x8, (block >> 2) * 8 + x8


FINAL = [
    [(device_of(c, b), final_target(c, b, j)[1]) for c in range(CH) for b in range(BLOCKS)]
    for j in range(ROUNDS)
]


def meta_table():
    meta = np.zeros((128, 2 + 2 * ROUNDS), np.int32)
    for c in range(CH):
        for b in range(BLOCKS):
            me = device_of(c, b)
            meta[me, 0] = b > 0
            meta[me, 1] = b < BLOCKS - 1
            for j in range(ROUNDS):
                x8, target = final_target(c, b, j)
                meta[me, 2 + j] = x8
                meta[target, 2 + ROUNDS + j] = c * 4 + (b & 3)
    return meta


def np_split(table):
    high = table.astype(np.float32).astype(jnp.bfloat16)
    low = (table - high.astype(np.float64)).astype(np.float32).astype(jnp.bfloat16)
    return high, low


def destripe_tables():
    i = np.arange(NX, dtype=np.float64)
    across = np.exp(-0.5 * ((i[:, None] - i[None, :]) / SIGMA_ACROSS) ** 2)
    across = across / across.sum(axis=1, keepdims=True)
    n = np.arange(NY, dtype=np.float64)
    c = np.minimum(n, NY - n)
    ring = np.exp(-0.5 * (c / SIGMA_ALONG) ** 2)
    ring = ring / ring.sum()
    along = ring[(np.arange(NY)[:, None] - np.arange(NY)[None, :]) % NY]
    h, q = NY // 2, NY // 4
    even = along[:h, :h] + along[:h, h:]
    odd = along[:h, :h] - along[:h, h:]
    even_even = even[:q, :q] + even[:q, q:]
    even_odd = even[:q, :q] - even[:q, q:]
    out = []
    for table in (across.T, odd, even_even, even_odd):
        out.extend(np_split(table))
    return out


def split(v):
    high = v.astype(BF16)
    return high, (v - high.astype(F32)).astype(BF16)


def dot(a, b):
    return jnp.dot(a, b, preferred_element_type=F32)


def dot3(a_high, a_low, b_high, b_low):
    return dot(a_high, b_high) + (dot(a_high, b_low) + dot(a_low, b_high))


def destripe_kernel(raw, ah, al, oh, ol, eeh, eel, eoh, eol, out, rt, sm, dh, dl, s1h, s1l, d1h, d1l):
    h, q = NY // 2, NY // 4

    @pl.loop(0, NY // 256)
    def _(i):
        r = pl.multiple_of(i * 256, 256)
        tile = raw[0, 0, :, pl.ds(r, 256)].T
        rt[pl.ds(r, 256), :] = tile
        th, tl = split(tile)
        sm[pl.ds(r, 256), :] = dot3(th, tl, ah[...], al[...])

    @pl.loop(0, q // 128)
    def _(i):
        r = pl.multiple_of(i * 128, 128)
        parts = [sm[pl.ds(r + m * q, 128), :] for m in range(4)]
        for m in range(2):
            hi, lo = split(0.5 * (parts[m] - parts[m + 2]))
            dh[pl.ds(r + m * q, 128), :] = hi
            dl[pl.ds(r + m * q, 128), :] = lo
        top = 0.5 * (parts[0] + parts[2])
        bottom = 0.5 * (parts[1] + parts[3])
        hi, lo = split(0.5 * (top + bottom))
        s1h[pl.ds(r, 128), :] = hi
        s1l[pl.ds(r, 128), :] = lo
        hi, lo = split(0.5 * (top - bottom))
        d1h[pl.ds(r, 128), :] = hi
        d1l[pl.ds(r, 128), :] = lo

    def emit(row, smooth):
        for m in range(8):
            x, yl, z, core = place(row // LINES + m)
            at = pl.ds(row + m * LINES, LINES)
            part = smooth[m * LINES : (m + 1) * LINES, :]
            clean = jnp.maximum(rt[at, :] - (sm[at, :] - part), 0.0)
            gx = (z * 2 + yl) * 2 + core
            out[gx, x, 0, 0:LINES, :] = clean[:, :128]
            out[gx, x, 0, LINES : 2 * LINES, :] = clean[:, 128:]

    for i in range(2):
        at = slice(i * 256, (i + 1) * 256)
        ee = dot3(eeh[at, :], eel[at, :], s1h[...], s1l[...])
        eo = dot3(eoh[at, :], eol[at, :], d1h[...], d1l[...])
        for m in range(2):
            row = m * q + i * 256
            even = ee + eo if m == 0 else ee - eo
            rows = slice(row, row + 256)
            odd = dot3(oh[rows, :], ol[rows, :], dh[...], dl[...])
            emit(row, even + odd)
            emit(h + row, even - odd)


def destripe(raw_stack):
    tables = [jnp.asarray(t) for t in destripe_tables()]
    whole = pl.BlockSpec(memory_space=pltpu.VMEM)
    return pl.pallas_call(
        destripe_kernel,
        grid=(CH,),
        in_specs=[pl.BlockSpec((1, 1, NX, NY), lambda c: (c, 0, 0, 0))] + [whole] * 8,
        out_specs=pl.BlockSpec((16, 4, 1, 64, 128), lambda c: (0, 0, c, 0, 0)),
        out_shape=jax.ShapeDtypeStruct((16, 4, CH, 64, 128), F32),
        scratch_shapes=[
            pltpu.VMEM((NY, NX), F32),
            pltpu.VMEM((NY, NX), F32),
            pltpu.VMEM((NY // 2, NX), BF16),
            pltpu.VMEM((NY // 2, NX), BF16),
        ]
        + [pltpu.VMEM((NY // 4, NX), BF16)] * 4,
        compiler_params=pltpu.CompilerParams(vmem_limit_bytes=60 * 1024 * 1024),
        name="destripe",
    )(raw_stack, *tables)


def band(weights, size):
    shape = (size, size)
    lag = lax.broadcasted_iota(jnp.int32, shape, 1) - lax.broadcasted_iota(jnp.int32, shape, 0)
    out = jnp.zeros(shape, F32)
    for k in range(TAPS):
        out = jnp.where(lag == k - HALF, weights[k], out)
    return out


def tables_kernel(taps, *outs):
    for way in range(2):
        z_table, x_table = outs[2 * way : 2 * way + 2]
        hi, lo = split(band(tap_list(taps, 0, 1 - way), NZ))
        for half in range(2):
            rows = slice(half * NZ, (half + 1) * NZ)
            z_table[rows, :NZ] = hi
            z_table[rows, NZ:] = lo
        hi, lo = split(band(tap_list(taps, 1, way), NX))
        x_table[:, :NX] = hi
        x_table[:, NX : 2 * NX] = hi
        x_table[:, 2 * NX :] = lo


def filter_tables(taps):
    shapes = [jax.ShapeDtypeStruct(s, BF16) for s in ((2 * NZ, 2 * NZ), (NX, 3 * NX))]
    outs = pl.pallas_call(
        tables_kernel,
        in_specs=[pl.BlockSpec(memory_space=pltpu.SMEM)],
        out_shape=shapes * 2,
        compiler_params=pltpu.CompilerParams(vmem_limit_bytes=VMEM_LIMIT),
        cost_estimate=pl.CostEstimate(flops=10**10, bytes_accessed=10**6, transcendentals=0),
        name="tables",
    )(taps)
    return outs[:2], outs[2:]


def tap_list(taps, axis, way):
    return [taps[axis, k if way == 0 else TAPS - 1 - k] for k in range(TAPS)]


def filter_z(v, z_table):
    hi, lo = split(v)
    both = dot(jnp.concatenate([hi, lo], axis=1), z_table)
    return both[:, :NZ] + both[:, NZ:]


def filter_zx(pair, z_table, x_table):
    v = filter_z(jnp.concatenate(pair, axis=0), z_table)
    hi, lo = split(jnp.concatenate([v[:NX], v[NX:]], axis=1))
    both = dot(x_table, jnp.concatenate([hi, lo, hi], axis=0))
    return both[:, :NZ], both[:, NZ:]


HALF_SHAPES = ((HALF, NX, NZ), (1, NX, NZ))


def store_pair(side, i, pair, outer, inner):
    for m in range(2):
        y = 2 * i + m
        if side == 0:
            ref, at = (inner, 0) if y == HALF else (outer, y)
        else:
            ref, at = (inner, 0) if y == 0 else (outer, y - 1)
        ref[at] = pair[m]


def calls(kernel, name, shapes, scratch=(), cost=None, **more):
    params = pltpu.CompilerParams(vmem_limit_bytes=VMEM_LIMIT)
    if cost:
        more["cost_estimate"] = pl.CostEstimate(flops=cost, bytes_accessed=10**6, transcendentals=0)
    return pl.pallas_call(
        kernel,
        out_shape=[jax.ShapeDtypeStruct(s, F32) for s in shapes],
        scratch_shapes=list(scratch),
        compiler_params=params,
        name=name,
        **more,
    )


WHOLE = pl.BlockSpec(memory_space=pltpu.VMEM)
SCALARS = pl.BlockSpec(memory_space=pltpu.SMEM)


def arrive_kernel(side, got, z_table, x_table, cleaned, outer, inner):
    for i in range(HL // 2):
        for m in range(2):
            for half in range(2):
                row = half * LINES + side * HL + 2 * i + m
                tile = got[pl.ds(row, NZ, stride=2 * LINES), :].T
                cleaned[2 * i + m, half * 128 : (half + 1) * 128, :] = tile
        lines = [cleaned[2 * i], cleaned[2 * i + 1]]
        store_pair(side, i, filter_zx(lines, z_table[...], x_table[...]), outer, inner)


def arrive(side, got, tables):
    return calls(
        functools.partial(arrive_kernel, side),
        f"arrive_{side}",
        ((HL, NX, NZ),) + HALF_SHAPES,
        in_specs=[WHOLE] * 3,
    )(got, *tables)


def own_kernel(way, side, taps, low, low_mid, high_mid, high, out):
    weights = [jnp.full((8, NZ), tap, F32) for tap in tap_list(taps, 2, way)]

    def line(j, at):
        if j < HALF:
            return low[j, at, :]
        if j < LINES - HALF:
            return (low_mid, high_mid)[j - HALF][0, at, :]
        return high[j - (LINES - HALF), at, :]

    @pl.loop(0, NX // 8)
    def _(t):
        at = pl.ds(pl.multiple_of(t * 8, 8), 8)
        for first in range(0, HL, 8):
            base = side * HL + first
            sums = [None] * 8
            for j in range(max(0, base - HALF), min(LINES, base + 8 + HALF)):
                v = line(j, at)
                for m in range(8):
                    k = j - (base + m) + HALF
                    if 0 <= k < TAPS:
                        term = weights[k] * v
                        sums[m] = term if sums[m] is None else sums[m] + term
            for m in range(8):
                out[first + m, at, :] = sums[m]


def own_lines(way, side, taps, halves):
    (low, low_mid), (high, high_mid) = halves
    return calls(
        functools.partial(own_kernel, way, side),
        f"own_lines_{side}",
        ((HL, NX, NZ),),
        cost=4 * 10**9,
        in_specs=[SCALARS] + [WHOLE] * 4,
    )(taps, low, low_mid, high_mid, high)[0]


def add_halo(way, side, taps, meta, partial, halo, at, use):
    weights = [jnp.full((8, NZ), tap, F32) for tap in tap_list(taps, 2, way)]
    there = meta[side] != 0
    for first in range(0, HL, 8):
        sums = [partial[first + m, at, :] for m in range(8)]
        for j in range(HALF):
            ks = [j - (first + m) if side == 0 else 2 * HL - 1 + j - (first + m) for m in range(8)]
            if any(0 <= k < TAPS for k in ks):
                v = jnp.where(there, halo[j, at, :], 0.0)
                for m in range(8):
                    if 0 <= ks[m] < TAPS:
                        sums[m] = sums[m] + weights[ks[m]] * v
        for m in range(8):
            use(first + m, sums[m])


def step_kernel(ratio, side, taps, meta, partial, halo, other, z_table, x_table, *rest):
    if ratio:
        outer, inner, work = rest
    else:
        work, outer, inner = rest

    @pl.loop(0, NX // 8)
    def _(t):
        at = pl.ds(pl.multiple_of(t * 8, 8), 8)

        def use(y, total):
            if ratio:
                work[y, at, :] = other[y, at, :] / (total + BACKGROUND)
            else:
                work[y, at, :] = other[y, at, :] * total

        add_halo(0 if ratio else 1, side, taps, meta, partial, halo, at, use)

    for i in range(HL // 2):
        lines = [work[2 * i], work[2 * i + 1]]
        store_pair(side, i, filter_zx(lines, z_table[...], x_table[...]), outer, inner)


def step(ratio, side, taps, meta, partial, halo, other, tables):
    return calls(
        functools.partial(step_kernel, ratio, side),
        f"ratio_step_{side}" if ratio else f"estimate_step_{side}",
        HALF_SHAPES if ratio else ((HL, NX, NZ),) + HALF_SHAPES,
        [pltpu.VMEM((HL, NX, NZ), F32)] if ratio else [],
        in_specs=[SCALARS] * 2 + [WHOLE] * 5,
    )(taps, meta, partial, halo, other, *tables)


def last_kernel(j, meta, taps, *refs):
    partials, halos, others, out = refs[:2], refs[2:4], refs[4:6], refs[6]

    @pl.loop(0, 4)
    def _(t):
        to = pl.ds(pl.multiple_of(t * 8, 8), 8)
        at = pl.ds(pl.multiple_of(meta[2 + j] * 32 + t * 8, 8), 8)
        for side in range(2):

            def use(y, total):
                out[side * HL + y, to, :] = others[side][y, at, :] * total

            add_halo(1, side, taps, meta, partials[side], halos[side], at, use)


def last(j, taps, meta, partials, halos, others):
    return calls(
        functools.partial(last_kernel, j),
        "last_step",
        ((LINES, 32, NZ),),
        in_specs=[SCALARS] * 2 + [WHOLE] * 6,
    )(meta, taps, *partials, *halos, *others)[0]


def leave_kernel(meta, *refs):
    parts, out, held = refs[:ROUNDS], refs[ROUNDS], refs[ROUNDS + 1]
    rows = LINES * 32
    for j in range(ROUNDS):
        base = meta[2 + ROUNDS + j] * rows

        @pl.loop(0, LINES, unroll=8)
        def _(y):
            held[pl.ds(pl.multiple_of(base + y * 32, 32), 32), :] = parts[j][y]

    @pl.loop(0, CH * 32, unroll=8)
    def _(i):
        start = (i // 32) * (128 * 32) + lax.rem(i, 32)
        tile = held[pl.ds(start, 128, stride=32), :].T
        out[pl.ds(start, 128, stride=32), :] = tile


def leave(meta, parts):
    return calls(
        leave_kernel,
        "leave",
        ((CH * NZ * 32, 128),),
        [pltpu.VMEM((CH * 128 * 32, NZ), F32)],
        in_specs=[SCALARS] + [WHOLE] * ROUNDS,
    )(meta, *parts)[0]


def local(raw_stack, psf_taps):
    me = lax.axis_index("gx") * 8 + lax.axis_index("gy")
    channel = lax.rem(lax.axis_index("gy"), 2)
    meta = lax.dynamic_index_in_dim(jnp.asarray(meta_table()), me, keepdims=False)
    taps = lax.dynamic_index_in_dim(psf_taps, channel, axis=1, keepdims=False)
    taps = taps / jnp.sum(taps, axis=1, keepdims=True)

    blocks = destripe(raw_stack).reshape(128, 64, 128)
    got = lax.all_to_all(blocks, AXES, split_axis=0, concat_axis=0, tiled=True)
    tables = filter_tables(taps)
    got = got.reshape(128 * 64, 128)
    cleaned, halves, halos = [None, None], [None, None], [None, None]

    def exchange(side):
        halos[1 - side] = lax.ppermute(halves[side][0], AXES, DOWN if side == 0 else UP)

    first = 0
    for side in (first, 1 - first):
        cleaned[side], *halves[side] = arrive(side, got, tables[0])
        exchange(side)

    estimate = list(cleaned)
    for blur in range(2 * ITERS):
        way = blur % 2
        first = 1 - first
        partials = [None, None]
        for side in (first, 1 - first):
            partials[side] = own_lines(way, side, taps, halves)
        if blur == 2 * ITERS - 1:
            parts = [last(j, taps, meta, partials, halos, estimate) for j in range(ROUNDS)]
            break
        arrived = list(halos)
        halves = [None, None]
        for side in (first, 1 - first):
            args = (side, taps, meta, partials[side], arrived[side])
            if way == 0:
                halves[side] = step(True, *args, cleaned[side], tables[1])
            else:
                estimate[side], *halves[side] = step(False, *args, estimate[side], tables[0])
            exchange(side)
    parts = [lax.ppermute(part, AXES, FINAL[j]) for j, part in enumerate(parts)]
    return leave(meta, parts).reshape(CH, NZ, 32, 128)


def solution(mesh):
    in_specs = (P(None, AXES, None, None), P())
    out_specs = P(None, None, "gy", "gx")
    return jax.shard_map(local, mesh=mesh, in_specs=in_specs, out_specs=out_specs, check_vma=False)
```

```python
import functools

import jax
import jax.numpy as jnp
import numpy as np
from jax import lax
from jax.experimental import pallas as pl
from jax.experimental.pallas import tpu as pltpu
from jax.sharding import PartitionSpec as P

CH, NZ, NX, NY = 2, 128, 256, 2048
TAPS, HALF = 31, 15
ITERS = 2
BACKGROUND = 0.5
SIGMA_ACROSS = 48.0
SIGMA_ALONG = 96.0

LINES = 32
BLOCKS = NY // LINES
AXES = ("gx", "gy")
F32, BF16 = jnp.float32, jnp.bfloat16
VMEM_LIMIT = 16 * 1024 * 1024
HL = LINES // 2


def rank(x, yh, yl, z, core):
    return ((z * 2 + yl) * 2 + core) * 8 + x * 2 + yh


def place(block):
    core, row, step = block & 1, block >> 3, (block >> 1) & 3
    z, k = row >> 1, row & 1
    return (step if k == 0 else 3 - step), k ^ (z & 1), z, core


def device_of(channel, block):
    x, yl, z, core = place(block)
    return rank(x, channel, yl, z, core)


UP = [(device_of(c, b), device_of(c, (b + 1) % BLOCKS)) for c in range(CH) for b in range(BLOCKS)]
DOWN = [(target, source) for source, target in UP]

ROUNDS = 8


def final_target(channel, block, j):
    x, _, _, core = place(block)
    xd = (x + 2 * core + (j & 3)) % 4
    x8 = 2 * xd + (channel ^ (j >> 2) ^ ((block >> 2) & 1))
    return x8, (block >> 2) * 8 + x8


FINAL = [
    [(device_of(c, b), final_target(c, b, j)[1]) for c in range(CH) for b in range(BLOCKS)]
    for j in range(ROUNDS)
]


def meta_table():
    meta = np.zeros((128, 4 + 2 * ROUNDS), np.int32)
    for c in range(CH):
        for b in range(BLOCKS):
            me = device_of(c, b)
            meta[me, 0] = b > 0
            meta[me, 1] = b < BLOCKS - 1
            for j in range(ROUNDS):
                x8, target = final_target(c, b, j)
                meta[me, 2 + j] = x8
                meta[target, 2 + ROUNDS + j] = b & 3
                meta[target, 2 + 2 * ROUNDS + (j >> 2)] = c
    return meta


def np_split(table):
    high = table.astype(np.float32).astype(jnp.bfloat16)
    low = (table - high.astype(np.float64)).astype(np.float32).astype(jnp.bfloat16)
    return high, low


def destripe_tables():
    i = np.arange(NX, dtype=np.float64)
    across = np.exp(-0.5 * ((i[:, None] - i[None, :]) / SIGMA_ACROSS) ** 2)
    across = across / across.sum(axis=1, keepdims=True)
    n = np.arange(NY, dtype=np.float64)
    c = np.minimum(n, NY - n)
    ring = np.exp(-0.5 * (c / SIGMA_ALONG) ** 2)
    ring = ring / ring.sum()
    along = ring[(np.arange(NY)[:, None] - np.arange(NY)[None, :]) % NY]
    h, q = NY // 2, NY // 4
    even = along[:h, :h] + along[:h, h:]
    odd = along[:h, :h] - along[:h, h:]
    even_even = even[:q, :q] + even[:q, q:]
    even_odd = even[:q, :q] - even[:q, q:]
    ah, al = np_split(across.T)
    return ah, al, np.stack(np_split(odd)), np.stack(np_split(even_even) + np_split(even_odd))


def split(v):
    high = v.astype(BF16)
    return high, (v - high.astype(F32)).astype(BF16)


def dot(a, b):
    return jnp.dot(a, b, preferred_element_type=F32)


def dot3(a_high, a_low, b_high, b_low):
    return dot(a_high, b_high) + (dot(a_high, b_low) + dot(a_low, b_high))


def destripe_kernel(raw, ah, al, odd_in, even_in, out, rt, sm, dh, dl, s1h, s1l, d1h, d1l, odd, even, sems):
    h, q = NY // 2, NY // 4
    copies = [
        pltpu.make_async_copy(odd_in, odd, sems.at[0]),
        pltpu.make_async_copy(even_in, even, sems.at[1]),
    ]

    @pl.when(pl.program_id(0) == 0)
    def _():
        for copy in copies:
            copy.start()

    @pl.loop(0, NY // 256, unroll=4)
    def _(i):
        r = pl.multiple_of(i * 256, 256)
        tile = raw[0, 0, :, pl.ds(r, 256)].T
        rt[pl.ds(r, 256), :] = tile
        th, tl = split(tile)
        sm[pl.ds(r, 256), :] = dot3(th, tl, ah[...], al[...])

    @pl.loop(0, q // 128)
    def _(i):
        r = pl.multiple_of(i * 128, 128)
        parts = [sm[pl.ds(r + m * q, 128), :] for m in range(4)]
        for m in range(2):
            hi, lo = split(0.5 * (parts[m] - parts[m + 2]))
            dh[pl.ds(r + m * q, 128), :] = hi
            dl[pl.ds(r + m * q, 128), :] = lo
        top = 0.5 * (parts[0] + parts[2])
        bottom = 0.5 * (parts[1] + parts[3])
        hi, lo = split(0.5 * (top + bottom))
        s1h[pl.ds(r, 128), :] = hi
        s1l[pl.ds(r, 128), :] = lo
        hi, lo = split(0.5 * (top - bottom))
        d1h[pl.ds(r, 128), :] = hi
        d1l[pl.ds(r, 128), :] = lo

    @pl.when(pl.program_id(0) == 0)
    def _():
        for copy in copies:
            copy.wait()

    def emit(row, smooth):
        for m in range(8):
            x, yl, z, core = place(row // LINES + m)
            at = pl.ds(row + m * LINES, LINES)
            part = smooth[m * LINES : (m + 1) * LINES, :]
            clean = jnp.maximum(rt[at, :] - (sm[at, :] - part), 0.0)
            gx = (z * 2 + yl) * 2 + core
            for side in range(2):
                for half in range(2):
                    to = (2 * side + half) * HL
                    tile = clean[side * HL : (side + 1) * HL, half * 128 : (half + 1) * 128]
                    out[gx, x, 0, to : to + HL, :] = tile

    for i in range(2):
        at = slice(i * 256, (i + 1) * 256)
        ee = dot3(even[0, at, :], even[1, at, :], s1h[...], s1l[...])
        eo = dot3(even[2, at, :], even[3, at, :], d1h[...], d1l[...])
        for m in range(2):
            row = m * q + i * 256
            rows = slice(row, row + 256)
            smooth_even = ee + eo if m == 0 else ee - eo
            smooth_odd = dot3(odd[0, rows, :], odd[1, rows, :], dh[...], dl[...])
            emit(row, smooth_even + smooth_odd)
            emit(h + row, smooth_even - smooth_odd)


def destripe(raw_stack):
    tables = [jnp.asarray(t) for t in destripe_tables()]
    whole, anywhere = (pl.BlockSpec(memory_space=m) for m in (pltpu.VMEM, pl.ANY))
    return pl.pallas_call(
        destripe_kernel,
        grid=(CH,),
        in_specs=[pl.BlockSpec((1, 1, NX, NY), lambda c: (c, 0, 0, 0)), whole, whole, anywhere, anywhere],
        out_specs=pl.BlockSpec((16, 4, 1, 64, 128), lambda c: (0, 0, c, 0, 0)),
        out_shape=jax.ShapeDtypeStruct((16, 4, CH, 64, 128), F32),
        scratch_shapes=[
            pltpu.VMEM((NY, NX), F32),
            pltpu.VMEM((NY, NX), F32),
            pltpu.VMEM((NY // 2, NX), BF16),
            pltpu.VMEM((NY // 2, NX), BF16),
        ]
        + [pltpu.VMEM((NY // 4, NX), BF16)] * 4
        + [
            pltpu.VMEM((2, NY // 2, NY // 2), BF16),
            pltpu.VMEM((4, NY // 4, NY // 4), BF16),
            pltpu.SemaphoreType.DMA((2,)),
        ],
        compiler_params=pltpu.CompilerParams(vmem_limit_bytes=60 * 1024 * 1024),
        name="destripe",
    )(raw_stack, *tables)


def band(weights, size):
    shape = (size, size)
    lag = lax.broadcasted_iota(jnp.int32, shape, 1) - lax.broadcasted_iota(jnp.int32, shape, 0)
    out = jnp.zeros(shape, F32)
    for k in range(TAPS):
        out = jnp.where(lag == k - HALF, weights[k], out)
    return out


def tables_kernel(taps, *outs):
    for way in range(2):
        z_table, x_table = outs[2 * way : 2 * way + 2]
        hi, lo = split(band(tap_list(taps, 0, 1 - way), NZ))
        for half in range(2):
            rows = slice(half * NZ, (half + 1) * NZ)
            z_table[rows, :NZ] = hi
            z_table[rows, NZ:] = lo
        hi, lo = split(band(tap_list(taps, 1, way), NX))
        x_table[:, :NX] = hi
        x_table[:, NX : 2 * NX] = hi
        x_table[:, 2 * NX :] = lo


def filter_tables(taps):
    shapes = [jax.ShapeDtypeStruct(s, BF16) for s in ((2 * NZ, 2 * NZ), (NX, 3 * NX))]
    outs = pl.pallas_call(
        tables_kernel,
        in_specs=[pl.BlockSpec(memory_space=pltpu.SMEM)],
        out_shape=shapes * 2,
        compiler_params=pltpu.CompilerParams(vmem_limit_bytes=VMEM_LIMIT),
        cost_estimate=pl.CostEstimate(flops=10**10, bytes_accessed=10**6, transcendentals=0),
        name="tables",
    )(taps)
    return outs[:2], outs[2:]


def tap_list(taps, axis, way):
    return [taps[axis, k if way == 0 else TAPS - 1 - k] for k in range(TAPS)]


def filter_z(v, z_table):
    hi, lo = split(v)
    return dot(jnp.concatenate([hi, lo], axis=1), z_table[:, :NZ]) + dot(hi, z_table[:NZ, NZ:])


def filter_zx(pair, z_table, x_table):
    v = filter_z(jnp.concatenate(pair, axis=0), z_table)
    hi, lo = split(jnp.concatenate([v[:NX], v[NX:]], axis=1))
    both = dot(x_table, jnp.concatenate([hi, lo, hi], axis=0))
    return both[:, :NZ], both[:, NZ:]


HALF_SHAPES = ((HALF, NX, NZ), (1, NX, NZ))


def store_pair(side, i, pair, outer, inner):
    for m in range(2):
        y = 2 * i + m
        if side == 0:
            ref, at = (inner, 0) if y == HALF else (outer, y)
        else:
            ref, at = (inner, 0) if y == 0 else (outer, y - 1)
        ref[at] = pair[m]


def calls(kernel, name, shapes, scratch=(), cost=None, **more):
    params = pltpu.CompilerParams(vmem_limit_bytes=VMEM_LIMIT)
    if cost:
        more["cost_estimate"] = pl.CostEstimate(flops=cost, bytes_accessed=10**6, transcendentals=0)
    return pl.pallas_call(
        kernel,
        out_shape=[jax.ShapeDtypeStruct(s, F32) for s in shapes],
        scratch_shapes=list(scratch),
        compiler_params=params,
        name=name,
        **more,
    )


WHOLE = pl.BlockSpec(memory_space=pltpu.VMEM)
SCALARS = pl.BlockSpec(memory_space=pltpu.SMEM)


def arrive_kernel(side, got, z_table, x_table, cleaned, outer, inner):
    for i in range(HL // 2):
        for m in range(2):
            for half in range(2):
                row = half * HL + 2 * i + m
                tile = got[pl.ds(row, NZ, stride=LINES), :].T
                cleaned[2 * i + m, half * 128 : (half + 1) * 128, :] = tile
        lines = [cleaned[2 * i], cleaned[2 * i + 1]]
        store_pair(side, i, filter_zx(lines, z_table[...], x_table[...]), outer, inner)


def arrive(side, got, tables):
    def kernel(got, *refs):
        arrive_kernel(side, got.reshape(NZ * LINES, 128), *refs)

    return calls(
        kernel,
        f"arrive_{side}",
        ((HL, NX, NZ),) + HALF_SHAPES,
        grid=(1,),
        in_specs=[pl.BlockSpec((NZ, LINES, 128), lambda i: (0, side, 0)), WHOLE, WHOLE],
        out_specs=[WHOLE] * 3,
    )(got, *tables)


def own_kernel(way, side, taps, low, low_mid, high_mid, high, out):
    weights = [jnp.full((8, NZ), tap, F32) for tap in tap_list(taps, 2, way)]

    def line(j, at):
        if j < HALF:
            return low[j, at, :]
        if j < LINES - HALF:
            return (low_mid, high_mid)[j - HALF][0, at, :]
        return high[j - (LINES - HALF), at, :]

    @pl.loop(0, NX // 8)
    def _(t):
        at = pl.ds(pl.multiple_of(t * 8, 8), 8)
        for first in range(0, HL, 8):
            base = side * HL + first
            sums = [None] * 8
            for j in range(max(0, base - HALF), min(LINES, base + 8 + HALF)):
                v = line(j, at)
                for m in range(8):
                    k = j - (base + m) + HALF
                    if 0 <= k < TAPS:
                        term = weights[k] * v
                        sums[m] = term if sums[m] is None else sums[m] + term
            for m in range(8):
                out[first + m, at, :] = sums[m]


def own_lines(way, side, taps, halves):
    (low, low_mid), (high, high_mid) = halves
    return calls(
        functools.partial(own_kernel, way, side),
        f"own_lines_{side}",
        ((HL, NX, NZ),),
        cost=4 * 10**9,
        in_specs=[SCALARS] + [WHOLE] * 4,
    )(taps, low, low_mid, high_mid, high)[0]


def add_halo(way, side, taps, meta, partial, halo, at, use):
    weights = [jnp.full((8, NZ), tap, F32) for tap in tap_list(taps, 2, way)]
    there = meta[side] != 0
    for first in range(0, HL, 8):
        sums = [partial[first + m, at, :] for m in range(8)]
        for j in range(HALF):
            ks = [j - (first + m) if side == 0 else 2 * HL - 1 + j - (first + m) for m in range(8)]
            if any(0 <= k < TAPS for k in ks):
                v = jnp.where(there, halo[j, at, :], 0.0)
                for m in range(8):
                    if 0 <= ks[m] < TAPS:
                        sums[m] = sums[m] + weights[ks[m]] * v
        for m in range(8):
            use(first + m, sums[m])


def step_kernel(ratio, side, taps, meta, partial, halo, other, z_table, x_table, *rest):
    if ratio:
        outer, inner, work = rest
    else:
        work, outer, inner = rest

    @pl.loop(0, NX // 8)
    def _(t):
        at = pl.ds(pl.multiple_of(t * 8, 8), 8)

        def use(y, total):
            if ratio:
                work[y, at, :] = other[y, at, :] / (total + BACKGROUND)
            else:
                work[y, at, :] = other[y, at, :] * total

        add_halo(0 if ratio else 1, side, taps, meta, partial, halo, at, use)

    for i in range(HL // 2):
        lines = [work[2 * i], work[2 * i + 1]]
        store_pair(side, i, filter_zx(lines, z_table[...], x_table[...]), outer, inner)


def step(ratio, side, taps, meta, partial, halo, other, tables):
    return calls(
        functools.partial(step_kernel, ratio, side),
        f"ratio_step_{side}" if ratio else f"estimate_step_{side}",
        HALF_SHAPES if ratio else ((HL, NX, NZ),) + HALF_SHAPES,
        [pltpu.VMEM((HL, NX, NZ), F32)] if ratio else [],
        in_specs=[SCALARS] * 2 + [WHOLE] * 5,
    )(taps, meta, partial, halo, other, *tables)


def last_kernel(j, meta, taps, *refs):
    partials, halos, others, out = refs[:2], refs[2:4], refs[4:6], refs[6]

    @pl.loop(0, 4)
    def _(t):
        to = pl.ds(pl.multiple_of(t * 8, 8), 8)
        at = pl.ds(pl.multiple_of(meta[2 + j] * 32 + t * 8, 8), 8)
        for side in range(2):

            def use(y, total):
                out[side * HL + y, to, :] = others[side][y, at, :] * total

            add_halo(1, side, taps, meta, partials[side], halos[side], at, use)


def last(j, taps, meta, partials, halos, others):
    return calls(
        functools.partial(last_kernel, j),
        "last_step",
        ((LINES, 32, NZ),),
        in_specs=[SCALARS] * 2 + [WHOLE] * 6,
    )(meta, taps, *partials, *halos, *others)[0]


def leave_kernel(group, meta, *refs):
    parts, out, held, turned, sem = refs[:4], refs[-4], refs[-3], refs[-2], refs[-1]
    for j in range(4):
        base = meta[2 + ROUNDS + 4 * group + j] * (LINES * 32)

        @pl.loop(0, LINES, unroll=8)
        def _(y):
            held[pl.ds(pl.multiple_of(base + y * 32, 32), 32), :] = parts[j][y]

    @pl.loop(0, 32, unroll=16)
    def _(i):
        turned[pl.ds(i, NZ, stride=32), :] = held[pl.ds(i, 128, stride=32), :].T

    rows = NZ * 32
    at = pl.ds(pl.multiple_of(meta[2 + 2 * ROUNDS + group] * rows, rows), rows)
    copy = pltpu.make_async_copy(turned, out.at[at, :], sem)
    copy.start()
    copy.wait()


def leave(group, meta, parts, out=None):
    rows = NZ * 32
    anywhere = pl.BlockSpec(memory_space=pl.ANY)
    return pl.pallas_call(
        functools.partial(leave_kernel, group),
        in_specs=[SCALARS] + [WHOLE] * 4 + ([] if out is None else [anywhere]),
        out_specs=anywhere,
        out_shape=jax.ShapeDtypeStruct((CH * rows, 128), F32),
        input_output_aliases={} if out is None else {5: 0},
        scratch_shapes=[pltpu.VMEM((rows, NZ), F32)] * 2 + [pltpu.SemaphoreType.DMA],
        compiler_params=pltpu.CompilerParams(vmem_limit_bytes=VMEM_LIMIT),
        name=f"leave_{group}",
    )(meta, *parts, *([] if out is None else [out]))


def local(raw_stack, psf_taps):
    me = lax.axis_index("gx") * 8 + lax.axis_index("gy")
    channel = lax.rem(lax.axis_index("gy"), 2)
    meta = lax.dynamic_index_in_dim(jnp.asarray(meta_table()), me, keepdims=False)
    taps = lax.dynamic_index_in_dim(psf_taps, channel, axis=1, keepdims=False)
    taps = taps / jnp.sum(taps, axis=1, keepdims=True)

    blocks = destripe(raw_stack).reshape(128, 64, 128)
    got = lax.all_to_all(blocks, AXES, split_axis=0, concat_axis=0, tiled=True)
    tables = filter_tables(taps)
    cleaned, halves, halos = [None, None], [None, None], [None, None]

    def exchange(side):
        halos[1 - side] = lax.ppermute(halves[side][0], AXES, DOWN if side == 0 else UP)

    first = 0
    for side in (first, 1 - first):
        cleaned[side], *halves[side] = arrive(side, got, tables[0])
        exchange(side)

    estimate = list(cleaned)
    for blur in range(2 * ITERS):
        way = blur % 2
        first = 1 - first
        partials = [None, None]
        for side in (first, 1 - first):
            partials[side] = own_lines(way, side, taps, halves)
        if blur == 2 * ITERS - 1:
            break
        arrived = list(halos)
        halves = [None, None]
        for side in (first, 1 - first):
            args = (side, taps, meta, partials[side], arrived[side])
            if way == 0:
                halves[side] = step(True, *args, cleaned[side], tables[1])
            else:
                estimate[side], *halves[side] = step(False, *args, estimate[side], tables[0])
            exchange(side)
    parts = []
    for j in range(ROUNDS):
        part = last(j, taps, meta, partials, halos, estimate)
        parts.append(lax.ppermute(part, AXES, FINAL[j]))
    out = leave(0, meta, parts[:4])
    out = leave(1, meta, parts[4:], out)
    return out.reshape(CH, NZ, 32, 128)


def solution(mesh):
    in_specs = (P(None, AXES, None, None), P())
    out_specs = P(None, None, "gy", "gx")
    return jax.shard_map(local, mesh=mesh, in_specs=in_specs, out_specs=out_specs, check_vma=False)
```

```python
import functools

import jax
import jax.numpy as jnp
import numpy as np
from jax import lax
from jax.experimental import pallas as pl
from jax.experimental.pallas import tpu as pltpu
from jax.sharding import PartitionSpec as P

CH, NZ, NX, NY = 2, 128, 256, 2048
TAPS, HALF = 31, 15
ITERS = 2
BACKGROUND = 0.5
SIGMA_ACROSS = 48.0
SIGMA_ALONG = 96.0

LINES = 32
BLOCKS = NY // LINES
AXES = ("gx", "gy")
F32, BF16 = jnp.float32, jnp.bfloat16
VMEM_LIMIT = 16 * 1024 * 1024
HL = LINES // 2


def rank(x, yh, yl, z, core):
    return ((z * 2 + yl) * 2 + core) * 8 + x * 2 + yh


def place(block):
    core, row, step = block & 1, block >> 3, (block >> 1) & 3
    z, k = row >> 1, row & 1
    return (step if k == 0 else 3 - step), k ^ (z & 1), z, core


def device_of(channel, block):
    x, yl, z, core = place(block)
    return rank(x, channel, yl, z, core)


UP = [(device_of(c, b), device_of(c, (b + 1) % BLOCKS)) for c in range(CH) for b in range(BLOCKS)]
DOWN = [(target, source) for source, target in UP]

ROUNDS = 8


def final_target(channel, block, j):
    x, _, _, core = place(block)
    xd = (x + 2 * core + (j & 3)) % 4
    x8 = 2 * xd + (channel ^ (j >> 2) ^ ((block >> 2) & 1))
    return x8, (block >> 2) * 8 + x8


FINAL = [
    [(device_of(c, b), final_target(c, b, j)[1]) for c in range(CH) for b in range(BLOCKS)]
    for j in range(ROUNDS)
]


def meta_table():
    meta = np.zeros((128, 4 + 2 * ROUNDS), np.int32)
    for c in range(CH):
        for b in range(BLOCKS):
            me = device_of(c, b)
            meta[me, 0] = b > 0
            meta[me, 1] = b < BLOCKS - 1
            for j in range(ROUNDS):
                x8, target = final_target(c, b, j)
                meta[me, 2 + j] = x8
                meta[target, 2 + ROUNDS + j] = b & 3
                meta[target, 2 + 2 * ROUNDS + (j >> 2)] = c
    return meta


def np_split(table):
    high = table.astype(np.float32).astype(jnp.bfloat16)
    low = (table - high.astype(np.float64)).astype(np.float32).astype(jnp.bfloat16)
    return high, low


def destripe_tables():
    i = np.arange(NX, dtype=np.float64)
    across = np.exp(-0.5 * ((i[:, None] - i[None, :]) / SIGMA_ACROSS) ** 2)
    across = across / across.sum(axis=1, keepdims=True)
    n = np.arange(NY, dtype=np.float64)
    c = np.minimum(n, NY - n)
    ring = np.exp(-0.5 * (c / SIGMA_ALONG) ** 2)
    ring = ring / ring.sum()
    along = ring[(np.arange(NY)[:, None] - np.arange(NY)[None, :]) % NY]
    h, q = NY // 2, NY // 4
    even = along[:h, :h] + along[:h, h:]
    odd = along[:h, :h] - along[:h, h:]
    even_even = even[:q, :q] + even[:q, q:]
    even_odd = even[:q, :q] - even[:q, q:]
    size = 256
    blocks = []
    for table in (odd, even_even, even_odd):
        count = table.shape[0] // size
        for d in range(count - 1, -count, -1):
            r, c = max(d, 0) * size, max(-d, 0) * size
            blocks.append(table[r : r + size, c : c + size])
    return np.stack(np_split(across.T)), np.stack(np_split(np.concatenate(blocks, axis=1)))


def split(v):
    high = v.astype(BF16)
    return high, (v - high.astype(F32)).astype(BF16)


def dot(a, b):
    return jnp.dot(a, b, preferred_element_type=F32)


def dot3(a_high, a_low, b_high, b_low):
    return dot(a_high, b_high) + (dot(a_high, b_low) + dot(a_low, b_high))


def destripe_kernel(raw_in, across_in, along_in, out_to, raw, across, along, out, rt, sm, dh, dl, s1h, s1l, d1h, d1l, in_sems, out_sems):
    h, q = NY // 2, NY // 4
    across_copy = pltpu.make_async_copy(across_in, across, in_sems.at[0])
    along_copy = pltpu.make_async_copy(along_in, along, in_sems.at[1])
    raw_copies = [
        pltpu.make_async_copy(raw_in.at[c, 0], raw.at[c], in_sems.at[2 + c]) for c in range(CH)
    ]
    across_copy.start()
    raw_copies[0].start()
    raw_copies[1].start()
    across_copy.wait()
    for c in range(CH):
        raw_copies[c].wait()
        if c == 0:
            along_copy.start()

        @pl.loop(0, NY // 256, unroll=4)
        def _(i):
            r = pl.multiple_of(i * 256, 256)
            tile = raw[c, :, pl.ds(r, 256)].T
            rt[c, pl.ds(r, 256), :] = tile
            th, tl = split(tile)
            sm[c, pl.ds(r, 256), :] = dot3(th, tl, across[0], across[1])

        @pl.loop(0, q // 128)
        def _(i):
            r = pl.multiple_of(i * 128, 128)
            parts = [sm[c, pl.ds(r + m * q, 128), :] for m in range(4)]
            for m in range(2):
                hi, lo = split(0.5 * (parts[m] - parts[m + 2]))
                dh[c, pl.ds(r + m * q, 128), :] = hi
                dl[c, pl.ds(r + m * q, 128), :] = lo
            top = 0.5 * (parts[0] + parts[2])
            bottom = 0.5 * (parts[1] + parts[3])
            hi, lo = split(0.5 * (top + bottom))
            s1h[c, pl.ds(r, 128), :] = hi
            s1l[c, pl.ds(r, 128), :] = lo
            hi, lo = split(0.5 * (top - bottom))
            d1h[c, pl.ds(r, 128), :] = hi
            d1l[c, pl.ds(r, 128), :] = lo

    along_copy.wait()
    out_copies = []

    def emit(c, row, smooth):
        for m in range(8):
            x, yl, z, core = place(row // LINES + m)
            at = pl.ds(row + m * LINES, LINES)
            part = smooth[m * LINES : (m + 1) * LINES, :]
            clean = jnp.maximum(rt[c, at, :] - (sm[c, at, :] - part), 0.0)
            gx = (z * 2 + yl) * 2 + core
            for half in range(2):
                tile = clean[:, half * 128 : (half + 1) * 128]
                out[c, gx, x, pl.ds(half, LINES, stride=2), :] = tile
        first = (z * 2 + yl) * 2
        copy = pltpu.make_async_copy(
            out.at[c, pl.ds(first, 2)], out_to.at[pl.ds(first, 2), :, c], out_sems.at[len(out_copies)]
        )
        copy.start()
        out_copies.append(copy)

    def window(first, block, count, high, low):
        at = slice(first + (count - 1 - block) * 256, first + (2 * count - 1 - block) * 256)
        return dot3(along[0, :, at], along[1, :, at], high, low)

    for c in range(CH):
        for i in range(2):
            ee = window(7 * 256, i, 2, s1h[c], s1l[c])
            eo = window(10 * 256, i, 2, d1h[c], d1l[c])
            for m in range(2):
                row = m * q + i * 256
                even = ee + eo if m == 0 else ee - eo
                odd = window(0, 2 * m + i, 4, dh[c], dl[c])
                emit(c, row, even + odd)
                emit(c, h + row, even - odd)
    for copy in out_copies:
        copy.wait()


def destripe(raw_stack):
    across, along = (jnp.asarray(t) for t in destripe_tables())
    anywhere = pl.BlockSpec(memory_space=pl.ANY)
    return pl.pallas_call(
        destripe_kernel,
        in_specs=[anywhere] * 3,
        out_specs=anywhere,
        out_shape=jax.ShapeDtypeStruct((16, 4, CH, 64, 128), F32),
        scratch_shapes=[
            pltpu.VMEM((CH, NX, NY), F32),
            pltpu.VMEM(across.shape, BF16),
            pltpu.VMEM(along.shape, BF16),
            pltpu.VMEM((CH, 16, 4, 64, 128), F32),
            pltpu.VMEM((CH, NY, NX), F32),
            pltpu.VMEM((CH, NY, NX), F32),
            pltpu.VMEM((CH, NY // 2, NX), BF16),
            pltpu.VMEM((CH, NY // 2, NX), BF16),
        ]
        + [pltpu.VMEM((CH, NY // 4, NX), BF16)] * 4
        + [pltpu.SemaphoreType.DMA((4,)), pltpu.SemaphoreType.DMA((16,))],
        compiler_params=pltpu.CompilerParams(vmem_limit_bytes=60 * 1024 * 1024),
        name="destripe",
    )(raw_stack, across, along)


def band(weights, size):
    shape = (size, size)
    lag = lax.broadcasted_iota(jnp.int32, shape, 1) - lax.broadcasted_iota(jnp.int32, shape, 0)
    out = jnp.zeros(shape, F32)
    for k in range(TAPS):
        out = jnp.where(lag == k - HALF, weights[k], out)
    return out


def tables_kernel(taps, *outs):
    for way in range(2):
        z_table, x_table = outs[2 * way : 2 * way + 2]
        hi, lo = split(band(tap_list(taps, 0, 1 - way), NZ))
        for half in range(2):
            rows = slice(half * NZ, (half + 1) * NZ)
            z_table[rows, :NZ] = hi
            z_table[rows, NZ:] = lo
        hi, lo = split(band(tap_list(taps, 1, way), NX))
        x_table[:, :NX] = hi
        x_table[:, NX : 2 * NX] = hi
        x_table[:, 2 * NX :] = lo


def filter_tables(taps):
    shapes = [jax.ShapeDtypeStruct(s, BF16) for s in ((2 * NZ, 2 * NZ), (NX, 3 * NX))]
    outs = pl.pallas_call(
        tables_kernel,
        in_specs=[pl.BlockSpec(memory_space=pltpu.SMEM)],
        out_shape=shapes * 2,
        compiler_params=pltpu.CompilerParams(vmem_limit_bytes=VMEM_LIMIT),
        cost_estimate=pl.CostEstimate(flops=10**10, bytes_accessed=10**6, transcendentals=0),
        name="tables",
    )(taps)
    return outs[:2], outs[2:]


def tap_list(taps, axis, way):
    return [taps[axis, k if way == 0 else TAPS - 1 - k] for k in range(TAPS)]


def filter_z(v, z_table):
    hi, lo = split(v)
    return dot(jnp.concatenate([hi, lo], axis=1), z_table[:, :NZ]) + dot(hi, z_table[:NZ, NZ:])


def filter_zx(pair, z_table, x_table):
    v = filter_z(jnp.concatenate(pair, axis=0), z_table)
    hi, lo = split(jnp.concatenate([v[:NX], v[NX:]], axis=1))
    both = dot(x_table, jnp.concatenate([hi, lo, hi], axis=0))
    return both[:, :NZ], both[:, NZ:]


HALF_SHAPES = ((HALF, NX, NZ), (1, NX, NZ))


def store_pair(side, i, pair, outer, inner):
    for m in range(2):
        y = 2 * i + m
        if side == 0:
            ref, at = (inner, 0) if y == HALF else (outer, y)
        else:
            ref, at = (inner, 0) if y == 0 else (outer, y - 1)
        ref[at] = pair[m]


def calls(kernel, name, shapes, scratch=(), cost=None, **more):
    params = pltpu.CompilerParams(vmem_limit_bytes=VMEM_LIMIT)
    if cost:
        more["cost_estimate"] = pl.CostEstimate(flops=cost, bytes_accessed=10**6, transcendentals=0)
    return pl.pallas_call(
        kernel,
        out_shape=[jax.ShapeDtypeStruct(s, F32) for s in shapes],
        scratch_shapes=list(scratch),
        compiler_params=params,
        name=name,
        **more,
    )


WHOLE = pl.BlockSpec(memory_space=pltpu.VMEM)
SCALARS = pl.BlockSpec(memory_space=pltpu.SMEM)


def arrive_kernel(side, got, z_table, x_table, cleaned, outer, inner):
    rows = got.reshape(NZ * LINES, 128)
    for i in range(HL // 2):
        for m in range(2):
            for half in range(2):
                row = 2 * (2 * i + m) + half
                tile = rows[pl.ds(row, NZ, stride=LINES), :].T
                cleaned[2 * i + m, half * 128 : (half + 1) * 128, :] = tile
        lines = [cleaned[2 * i], cleaned[2 * i + 1]]
        store_pair(side, i, filter_zx(lines, z_table[...], x_table[...]), outer, inner)


def arrive(side, got, tables):
    return calls(
        functools.partial(arrive_kernel, side),
        f"arrive_{side}",
        ((HL, NX, NZ),) + HALF_SHAPES,
        grid=(1,),
        in_specs=[pl.BlockSpec((NZ, LINES, 128), lambda i: (0, side, 0)), WHOLE, WHOLE],
        out_specs=[WHOLE] * 3,
    )(got, *tables)


def own_kernel(way, side, taps, low, low_mid, high_mid, high, out):
    weights = [jnp.full((8, NZ), tap, F32) for tap in tap_list(taps, 2, way)]

    def line(j, at):
        if j < HALF:
            return low[j, at, :]
        if j < LINES - HALF:
            return (low_mid, high_mid)[j - HALF][0, at, :]
        return high[j - (LINES - HALF), at, :]

    @pl.loop(0, NX // 8)
    def _(t):
        at = pl.ds(pl.multiple_of(t * 8, 8), 8)
        for first in range(0, HL, 8):
            base = side * HL + first
            sums = [None] * 8
            for j in range(max(0, base - HALF), min(LINES, base + 8 + HALF)):
                v = line(j, at)
                for m in range(8):
                    k = j - (base + m) + HALF
                    if 0 <= k < TAPS:
                        term = weights[k] * v
                        sums[m] = term if sums[m] is None else sums[m] + term
            for m in range(8):
                out[first + m, at, :] = sums[m]


def own_lines(way, side, taps, halves):
    (low, low_mid), (high, high_mid) = halves
    return calls(
        functools.partial(own_kernel, way, side),
        f"own_lines_{side}",
        ((HL, NX, NZ),),
        cost=4 * 10**9,
        in_specs=[SCALARS] + [WHOLE] * 4,
    )(taps, low, low_mid, high_mid, high)[0]


def add_halo(way, side, taps, meta, partial, halo, at, use):
    weights = [jnp.full((8, NZ), tap, F32) for tap in tap_list(taps, 2, way)]
    there = meta[side] != 0
    for first in range(0, HL, 8):
        sums = [partial[first + m, at, :] for m in range(8)]
        for j in range(HALF):
            ks = [j - (first + m) if side == 0 else 2 * HL - 1 + j - (first + m) for m in range(8)]
            if any(0 <= k < TAPS for k in ks):
                v = jnp.where(there, halo[j, at, :], 0.0)
                for m in range(8):
                    if 0 <= ks[m] < TAPS:
                        sums[m] = sums[m] + weights[ks[m]] * v
        for m in range(8):
            use(first + m, sums[m])


def step_kernel(ratio, side, taps, meta, partial, halo, other, z_table, x_table, *rest):
    if ratio:
        outer, inner, work = rest
    else:
        work, outer, inner = rest

    @pl.loop(0, NX // 8)
    def _(t):
        at = pl.ds(pl.multiple_of(t * 8, 8), 8)

        def use(y, total):
            if ratio:
                work[y, at, :] = other[y, at, :] / (total + BACKGROUND)
            else:
                work[y, at, :] = other[y, at, :] * total

        add_halo(0 if ratio else 1, side, taps, meta, partial, halo, at, use)

    for i in range(HL // 2):
        lines = [work[2 * i], work[2 * i + 1]]
        store_pair(side, i, filter_zx(lines, z_table[...], x_table[...]), outer, inner)


def step(ratio, side, taps, meta, partial, halo, other, tables):
    return calls(
        functools.partial(step_kernel, ratio, side),
        f"ratio_step_{side}" if ratio else f"estimate_step_{side}",
        HALF_SHAPES if ratio else ((HL, NX, NZ),) + HALF_SHAPES,
        [pltpu.VMEM((HL, NX, NZ), F32)] if ratio else [],
        in_specs=[SCALARS] * 2 + [WHOLE] * 5,
    )(taps, meta, partial, halo, other, *tables)


def last_kernel(j, meta, taps, *refs):
    partials, halos, others, out = refs[:2], refs[2:4], refs[4:6], refs[6]

    @pl.loop(0, 4)
    def _(t):
        to = pl.ds(pl.multiple_of(t * 8, 8), 8)
        at = pl.ds(pl.multiple_of(meta[2 + j] * 32 + t * 8, 8), 8)
        for side in range(2):

            def use(y, total):
                out[side * HL + y, to, :] = others[side][y, at, :] * total

            add_halo(1, side, taps, meta, partials[side], halos[side], at, use)


def last(j, taps, meta, partials, halos, others):
    return calls(
        functools.partial(last_kernel, j),
        "last_step",
        ((LINES, 32, NZ),),
        in_specs=[SCALARS] * 2 + [WHOLE] * 6,
    )(meta, taps, *partials, *halos, *others)[0]


def leave_kernel(group, meta, *refs):
    parts, out, held, turned, sem = refs[:4], refs[-4], refs[-3], refs[-2], refs[-1]
    for j in range(4):
        base = meta[2 + ROUNDS + 4 * group + j] * (LINES * 32)

        @pl.loop(0, LINES, unroll=8)
        def _(y):
            held[pl.ds(pl.multiple_of(base + y * 32, 32), 32), :] = parts[j][y]

    @pl.loop(0, 32, unroll=16)
    def _(i):
        turned[pl.ds(i, NZ, stride=32), :] = held[pl.ds(i, 128, stride=32), :].T

    rows = NZ * 32
    at = pl.ds(pl.multiple_of(meta[2 + 2 * ROUNDS + group] * rows, rows), rows)
    copy = pltpu.make_async_copy(turned, out.at[at, :], sem)
    copy.start()
    copy.wait()


def leave(group, meta, parts, out=None):
    rows = NZ * 32
    anywhere = pl.BlockSpec(memory_space=pl.ANY)
    return pl.pallas_call(
        functools.partial(leave_kernel, group),
        in_specs=[SCALARS] + [WHOLE] * 4 + ([] if out is None else [anywhere]),
        out_specs=anywhere,
        out_shape=jax.ShapeDtypeStruct((CH * rows, 128), F32),
        input_output_aliases={} if out is None else {5: 0},
        scratch_shapes=[pltpu.VMEM((rows, NZ), F32)] * 2 + [pltpu.SemaphoreType.DMA],
        compiler_params=pltpu.CompilerParams(vmem_limit_bytes=VMEM_LIMIT),
        name=f"leave_{group}",
    )(meta, *parts, *([] if out is None else [out]))


def local(raw_stack, psf_taps):
    me = lax.axis_index("gx") * 8 + lax.axis_index("gy")
    channel = lax.rem(lax.axis_index("gy"), 2)
    meta = lax.dynamic_index_in_dim(jnp.asarray(meta_table()), me, keepdims=False)
    taps = lax.dynamic_index_in_dim(psf_taps, channel, axis=1, keepdims=False)
    taps = taps / jnp.sum(taps, axis=1, keepdims=True)

    blocks = destripe(raw_stack).reshape(128, 64, 128)
    got = lax.all_to_all(blocks, AXES, split_axis=0, concat_axis=0, tiled=True)
    tables = filter_tables(taps)
    cleaned, halves, halos = [None, None], [None, None], [None, None]

    def exchange(side):
        halos[1 - side] = lax.ppermute(halves[side][0], AXES, DOWN if side == 0 else UP)

    first = 0
    for side in (first, 1 - first):
        cleaned[side], *halves[side] = arrive(side, got, tables[0])
        exchange(side)

    estimate = list(cleaned)
    for blur in range(2 * ITERS):
        way = blur % 2
        first = 1 - first
        partials = [None, None]
        for side in (first, 1 - first):
            partials[side] = own_lines(way, side, taps, halves)
        if blur == 2 * ITERS - 1:
            break
        arrived = list(halos)
        halves = [None, None]
        for side in (first, 1 - first):
            args = (side, taps, meta, partials[side], arrived[side])
            if way == 0:
                halves[side] = step(True, *args, cleaned[side], tables[1])
            else:
                estimate[side], *halves[side] = step(False, *args, estimate[side], tables[0])
            exchange(side)
    parts = []
    for j in range(ROUNDS):
        part = last(j, taps, meta, partials, halos, estimate)
        parts.append(lax.ppermute(part, AXES, FINAL[j]))
    out = leave(0, meta, parts[:4])
    out = leave(1, meta, parts[4:], out)
    return out.reshape(CH, NZ, 32, 128)


def solution(mesh):
    in_specs = (P(None, AXES, None, None), P())
    out_specs = P(None, None, "gy", "gx")
    return jax.shard_map(local, mesh=mesh, in_specs=in_specs, out_specs=out_specs, check_vma=False)
```

```python
import functools

import jax
import jax.numpy as jnp
import numpy as np
from jax import lax
from jax.experimental import pallas as pl
from jax.experimental.pallas import tpu as pltpu
from jax.sharding import PartitionSpec as P

CH, NZ, NX, NY = 2, 128, 256, 2048
TAPS, HALF = 31, 15
ITERS = 2
BACKGROUND = 0.5
SIGMA_ACROSS = 48.0
SIGMA_ALONG = 96.0

LINES = 32
BLOCKS = NY // LINES
AXES = ("gx", "gy")
F32, BF16 = jnp.float32, jnp.bfloat16
VMEM_LIMIT = 16 * 1024 * 1024
HL = LINES // 2


def rank(x, yh, yl, z, core):
    return ((z * 2 + yl) * 2 + core) * 8 + x * 2 + yh


def place(block):
    core, row, step = block & 1, block >> 3, (block >> 1) & 3
    z, k = row >> 1, row & 1
    return (step if k == 0 else 3 - step), k ^ (z & 1), z, core


def device_of(channel, block):
    x, yl, z, core = place(block)
    return rank(x, channel, yl, z, core)


UP = [(device_of(c, b), device_of(c, (b + 1) % BLOCKS)) for c in range(CH) for b in range(BLOCKS)]
DOWN = [(target, source) for source, target in UP]

ROUNDS = 8


def final_target(channel, block, j):
    x, _, _, core = place(block)
    xd = (x + 2 * core + (1, 3, 0, 2)[j & 3]) % 4
    x8 = 2 * xd + (channel ^ (j >> 2) ^ ((block >> 2) & 1))
    return x8, (block >> 2) * 8 + x8


FINAL = [
    [(device_of(c, b), final_target(c, b, j)[1]) for c in range(CH) for b in range(BLOCKS)]
    for j in range(ROUNDS)
]


def meta_table():
    meta = np.zeros((128, 4 + 2 * ROUNDS), np.int32)
    for c in range(CH):
        for b in range(BLOCKS):
            me = device_of(c, b)
            meta[me, 0] = b > 0
            meta[me, 1] = b < BLOCKS - 1
            for j in range(ROUNDS):
                x8, target = final_target(c, b, j)
                meta[me, 2 + j] = x8
                meta[target, 2 + ROUNDS + j] = b & 3
                meta[target, 2 + 2 * ROUNDS + (j >> 2)] = c
    return meta


def np_split(table):
    high = table.astype(np.float32).astype(jnp.bfloat16)
    low = (table - high.astype(np.float64)).astype(np.float32).astype(jnp.bfloat16)
    return high, low


def destripe_tables():
    i = np.arange(NX, dtype=np.float64)
    across = np.exp(-0.5 * ((i[:, None] - i[None, :]) / SIGMA_ACROSS) ** 2)
    across = across / across.sum(axis=1, keepdims=True)
    n = np.arange(NY, dtype=np.float64)
    c = np.minimum(n, NY - n)
    ring = np.exp(-0.5 * (c / SIGMA_ALONG) ** 2)
    ring = ring / ring.sum()
    along = ring[(np.arange(NY)[:, None] - np.arange(NY)[None, :]) % NY]
    h, q = NY // 2, NY // 4
    even = along[:h, :h] + along[:h, h:]
    odd = along[:h, :h] - along[:h, h:]
    even_even = even[:q, :q] + even[:q, q:]
    even_odd = even[:q, :q] - even[:q, q:]
    size = 256
    blocks = []
    for table in (odd, even_even, even_odd):
        count = table.shape[0] // size
        for d in range(count - 1, -count, -1):
            r, c = max(d, 0) * size, max(-d, 0) * size
            blocks.append(table[r : r + size, c : c + size])
    return np.stack(np_split(across.T)), np.stack(np_split(np.concatenate(blocks, axis=1)))


def split(v):
    high = v.astype(BF16)
    return high, (v - high.astype(F32)).astype(BF16)


def dot(a, b):
    return jnp.dot(a, b, preferred_element_type=F32)


def dot3(a_high, a_low, b_high, b_low):
    return dot(a_high, b_high) + (dot(a_high, b_low) + dot(a_low, b_high))


def destripe_kernel(raw_in, across_in, along_in, out_to, raw, across, along, out, rt, sm, dh, dl, s1h, s1l, d1h, d1l, in_sems, out_sems):
    h, q = NY // 2, NY // 4
    across_copy = pltpu.make_async_copy(across_in, across, in_sems.at[0])
    along_copy = pltpu.make_async_copy(along_in, along, in_sems.at[1])
    raw_copies = [
        pltpu.make_async_copy(raw_in.at[c, 0], raw.at[c], in_sems.at[2 + c]) for c in range(CH)
    ]
    across_copy.start()
    raw_copies[0].start()
    raw_copies[1].start()
    across_copy.wait()
    for c in range(CH):
        raw_copies[c].wait()
        if c == 0:
            along_copy.start()

        @pl.loop(0, NY // 256, unroll=4)
        def _(i):
            r = pl.multiple_of(i * 256, 256)
            tile = raw[c, :, pl.ds(r, 256)].T
            rt[c, pl.ds(r, 256), :] = tile
            th, tl = split(tile)
            sm[c, pl.ds(r, 256), :] = dot3(th, tl, across[0], across[1])

        @pl.loop(0, q // 128)
        def _(i):
            r = pl.multiple_of(i * 128, 128)
            parts = [sm[c, pl.ds(r + m * q, 128), :] for m in range(4)]
            for m in range(2):
                hi, lo = split(0.5 * (parts[m] - parts[m + 2]))
                dh[c, pl.ds(r + m * q, 128), :] = hi
                dl[c, pl.ds(r + m * q, 128), :] = lo
            top = 0.5 * (parts[0] + parts[2])
            bottom = 0.5 * (parts[1] + parts[3])
            hi, lo = split(0.5 * (top + bottom))
            s1h[c, pl.ds(r, 128), :] = hi
            s1l[c, pl.ds(r, 128), :] = lo
            hi, lo = split(0.5 * (top - bottom))
            d1h[c, pl.ds(r, 128), :] = hi
            d1l[c, pl.ds(r, 128), :] = lo

    along_copy.wait()
    out_copies = []

    def emit(c, row, smooth):
        for m in range(8):
            x, yl, z, core = place(row // LINES + m)
            at = pl.ds(row + m * LINES, LINES)
            part = smooth[m * LINES : (m + 1) * LINES, :]
            clean = jnp.maximum(rt[c, at, :] - (sm[c, at, :] - part), 0.0)
            gx = (z * 2 + yl) * 2 + core
            for half in range(2):
                tile = clean[:, half * 128 : (half + 1) * 128]
                out[c, gx, x, pl.ds(half, LINES, stride=2), :] = tile
        first = (z * 2 + yl) * 2
        copy = pltpu.make_async_copy(
            out.at[c, pl.ds(first, 2)], out_to.at[pl.ds(first, 2), :, c], out_sems.at[len(out_copies)]
        )
        copy.start()
        out_copies.append(copy)

    def window(first, block, count, high, low):
        at = slice(first + (count - 1 - block) * 256, first + (2 * count - 1 - block) * 256)
        return dot3(along[0, :, at], along[1, :, at], high, low)

    for c in range(CH):
        for i in range(2):
            ee = window(7 * 256, i, 2, s1h[c], s1l[c])
            eo = window(10 * 256, i, 2, d1h[c], d1l[c])
            for m in range(2):
                row = m * q + i * 256
                even = ee + eo if m == 0 else ee - eo
                odd = window(0, 2 * m + i, 4, dh[c], dl[c])
                emit(c, row, even + odd)
                emit(c, h + row, even - odd)
    for copy in out_copies:
        copy.wait()


def destripe(raw_stack):
    across, along = (jnp.asarray(t) for t in destripe_tables())
    anywhere = pl.BlockSpec(memory_space=pl.ANY)
    return pl.pallas_call(
        destripe_kernel,
        in_specs=[anywhere] * 3,
        out_specs=anywhere,
        out_shape=jax.ShapeDtypeStruct((16, 4, CH, 64, 128), F32),
        scratch_shapes=[
            pltpu.VMEM((CH, NX, NY), F32),
            pltpu.VMEM(across.shape, BF16),
            pltpu.VMEM(along.shape, BF16),
            pltpu.VMEM((CH, 16, 4, 64, 128), F32),
            pltpu.VMEM((CH, NY, NX), F32),
            pltpu.VMEM((CH, NY, NX), F32),
            pltpu.VMEM((CH, NY // 2, NX), BF16),
            pltpu.VMEM((CH, NY // 2, NX), BF16),
        ]
        + [pltpu.VMEM((CH, NY // 4, NX), BF16)] * 4
        + [pltpu.SemaphoreType.DMA((4,)), pltpu.SemaphoreType.DMA((16,))],
        compiler_params=pltpu.CompilerParams(vmem_limit_bytes=60 * 1024 * 1024),
        name="destripe",
    )(raw_stack, across, along)


def band(weights, size):
    shape = (size, size)
    lag = lax.broadcasted_iota(jnp.int32, shape, 1) - lax.broadcasted_iota(jnp.int32, shape, 0)
    out = jnp.zeros(shape, F32)
    for k in range(TAPS):
        out = jnp.where(lag == k - HALF, weights[k], out)
    return out


def tables_kernel(taps, *outs):
    for way in range(2):
        z_table, x_table = outs[2 * way : 2 * way + 2]
        hi, lo = split(band(tap_list(taps, 0, 1 - way), NZ))
        for half in range(2):
            rows = slice(half * NZ, (half + 1) * NZ)
            z_table[rows, :NZ] = hi
            z_table[rows, NZ:] = lo
        hi, lo = split(band(tap_list(taps, 1, way), NX))
        x_table[:, :NX] = hi
        x_table[:, NX : 2 * NX] = hi
        x_table[:, 2 * NX :] = lo


def filter_tables(taps):
    shapes = [jax.ShapeDtypeStruct(s, BF16) for s in ((2 * NZ, 2 * NZ), (NX, 3 * NX))]
    outs = pl.pallas_call(
        tables_kernel,
        in_specs=[pl.BlockSpec(memory_space=pltpu.SMEM)],
        out_shape=shapes * 2,
        compiler_params=pltpu.CompilerParams(vmem_limit_bytes=VMEM_LIMIT),
        cost_estimate=pl.CostEstimate(flops=10**10, bytes_accessed=10**6, transcendentals=0),
        name="tables",
    )(taps)
    return outs[:2], outs[2:]


def tap_list(taps, axis, way):
    return [taps[axis, k if way == 0 else TAPS - 1 - k] for k in range(TAPS)]


def filter_z(v, z_table):
    hi, lo = split(v)
    return dot(jnp.concatenate([hi, lo], axis=1), z_table[:, :NZ]) + dot(hi, z_table[:NZ, NZ:])


def filter_zx(pair, z_table, x_table):
    v = filter_z(jnp.concatenate(pair, axis=0), z_table)
    hi, lo = split(jnp.concatenate([v[:NX], v[NX:]], axis=1))
    both = dot(x_table, jnp.concatenate([hi, lo, hi], axis=0))
    return both[:, :NZ], both[:, NZ:]


HALF_SHAPES = ((HALF, NX, NZ), (1, NX, NZ))


def store_pair(side, i, pair, outer, inner):
    for m in range(2):
        y = 2 * i + m
        if side == 0:
            ref, at = (inner, 0) if y == HALF else (outer, y)
        else:
            ref, at = (inner, 0) if y == 0 else (outer, y - 1)
        ref[at] = pair[m]


def calls(kernel, name, shapes, scratch=(), cost=None, **more):
    params = pltpu.CompilerParams(vmem_limit_bytes=VMEM_LIMIT)
    if cost:
        more["cost_estimate"] = pl.CostEstimate(flops=cost, bytes_accessed=10**6, transcendentals=0)
    return pl.pallas_call(
        kernel,
        out_shape=[jax.ShapeDtypeStruct(s, F32) for s in shapes],
        scratch_shapes=list(scratch),
        compiler_params=params,
        name=name,
        **more,
    )


WHOLE = pl.BlockSpec(memory_space=pltpu.VMEM)
SCALARS = pl.BlockSpec(memory_space=pltpu.SMEM)


def arrive_kernel(side, got, z_table, x_table, cleaned, outer, inner):
    rows = got.reshape(NZ * LINES, 128)
    for i in range(HL // 2):
        for m in range(2):
            for half in range(2):
                row = 2 * (2 * i + m) + half
                tile = rows[pl.ds(row, NZ, stride=LINES), :].T
                cleaned[2 * i + m, half * 128 : (half + 1) * 128, :] = tile
        lines = [cleaned[2 * i], cleaned[2 * i + 1]]
        store_pair(side, i, filter_zx(lines, z_table[...], x_table[...]), outer, inner)


def arrive(side, got, tables):
    return calls(
        functools.partial(arrive_kernel, side),
        f"arrive_{side}",
        ((HL, NX, NZ),) + HALF_SHAPES,
        grid=(1,),
        in_specs=[pl.BlockSpec((NZ, LINES, 128), lambda i: (0, side, 0)), WHOLE, WHOLE],
        out_specs=[WHOLE] * 3,
    )(got, *tables)


def own_kernel(way, side, taps, low, low_mid, high_mid, high, out):
    weights = [jnp.full((8, NZ), tap, F32) for tap in tap_list(taps, 2, way)]

    def line(j, at):
        if j < HALF:
            return low[j, at, :]
        if j < LINES - HALF:
            return (low_mid, high_mid)[j - HALF][0, at, :]
        return high[j - (LINES - HALF), at, :]

    @pl.loop(0, NX // 8)
    def _(t):
        at = pl.ds(pl.multiple_of(t * 8, 8), 8)
        for first in range(0, HL, 8):
            base = side * HL + first
            sums = [None] * 8
            for j in range(max(0, base - HALF), min(LINES, base + 8 + HALF)):
                v = line(j, at)
                for m in range(8):
                    k = j - (base + m) + HALF
                    if 0 <= k < TAPS:
                        term = weights[k] * v
                        sums[m] = term if sums[m] is None else sums[m] + term
            for m in range(8):
                out[first + m, at, :] = sums[m]


def own_lines(way, side, taps, halves):
    (low, low_mid), (high, high_mid) = halves
    return calls(
        functools.partial(own_kernel, way, side),
        f"own_lines_{side}",
        ((HL, NX, NZ),),
        cost=4 * 10**9,
        in_specs=[SCALARS] + [WHOLE] * 4,
    )(taps, low, low_mid, high_mid, high)[0]


def add_halo(way, side, taps, meta, partial, halo, at, use):
    weights = [jnp.full((8, NZ), tap, F32) for tap in tap_list(taps, 2, way)]
    there = meta[side] != 0
    for first in range(0, HL, 8):
        sums = [partial[first + m, at, :] for m in range(8)]
        for j in range(HALF):
            ks = [j - (first + m) if side == 0 else 2 * HL - 1 + j - (first + m) for m in range(8)]
            if any(0 <= k < TAPS for k in ks):
                v = jnp.where(there, halo[j, at, :], 0.0)
                for m in range(8):
                    if 0 <= ks[m] < TAPS:
                        sums[m] = sums[m] + weights[ks[m]] * v
        for m in range(8):
            use(first + m, sums[m])


def step_kernel(ratio, side, taps, meta, partial, halo, other, z_table, x_table, *rest):
    if ratio:
        outer, inner, work = rest
    else:
        work, outer, inner = rest

    @pl.loop(0, NX // 8)
    def _(t):
        at = pl.ds(pl.multiple_of(t * 8, 8), 8)

        def use(y, total):
            if ratio:
                work[y, at, :] = other[y, at, :] / (total + BACKGROUND)
            else:
                work[y, at, :] = other[y, at, :] * total

        add_halo(0 if ratio else 1, side, taps, meta, partial, halo, at, use)

    for i in range(HL // 2):
        lines = [work[2 * i], work[2 * i + 1]]
        store_pair(side, i, filter_zx(lines, z_table[...], x_table[...]), outer, inner)


def step(ratio, side, taps, meta, partial, halo, other, tables):
    return calls(
        functools.partial(step_kernel, ratio, side),
        f"ratio_step_{side}" if ratio else f"estimate_step_{side}",
        HALF_SHAPES if ratio else ((HL, NX, NZ),) + HALF_SHAPES,
        [pltpu.VMEM((HL, NX, NZ), F32)] if ratio else [],
        in_specs=[SCALARS] * 2 + [WHOLE] * 5,
    )(taps, meta, partial, halo, other, *tables)


def last_kernel(j, meta, taps, *refs):
    partials, halos, others, out = refs[:2], refs[2:4], refs[4:6], refs[6]

    @pl.loop(0, 4)
    def _(t):
        to = pl.ds(pl.multiple_of(t * 8, 8), 8)
        at = pl.ds(pl.multiple_of(meta[2 + j] * 32 + t * 8, 8), 8)
        for side in range(2):

            def use(y, total):
                out[side * HL + y, to, :] = others[side][y, at, :] * total

            add_halo(1, side, taps, meta, partials[side], halos[side], at, use)


def last(j, taps, meta, partials, halos, others):
    return calls(
        functools.partial(last_kernel, j),
        "last_step",
        ((LINES, 32, NZ),),
        in_specs=[SCALARS] * 2 + [WHOLE] * 6,
    )(meta, taps, *partials, *halos, *others)[0]


def leave_kernel(group, meta, *refs):
    parts, out, held, turned, sem = refs[:4], refs[-4], refs[-3], refs[-2], refs[-1]
    for j in range(4):
        base = meta[2 + ROUNDS + 4 * group + j] * (LINES * 32)

        @pl.loop(0, LINES, unroll=8)
        def _(y):
            held[pl.ds(pl.multiple_of(base + y * 32, 32), 32), :] = parts[j][y]

    @pl.loop(0, 32, unroll=16)
    def _(i):
        turned[pl.ds(i, NZ, stride=32), :] = held[pl.ds(i, 128, stride=32), :].T

    rows = NZ * 32
    at = pl.ds(pl.multiple_of(meta[2 + 2 * ROUNDS + group] * rows, rows), rows)
    copy = pltpu.make_async_copy(turned, out.at[at, :], sem)
    copy.start()
    copy.wait()


def leave(group, meta, parts, out=None):
    rows = NZ * 32
    anywhere = pl.BlockSpec(memory_space=pl.ANY)
    return pl.pallas_call(
        functools.partial(leave_kernel, group),
        in_specs=[SCALARS] + [WHOLE] * 4 + ([] if out is None else [anywhere]),
        out_specs=anywhere,
        out_shape=jax.ShapeDtypeStruct((CH * rows, 128), F32),
        input_output_aliases={} if out is None else {5: 0},
        scratch_shapes=[pltpu.VMEM((rows, NZ), F32)] * 2 + [pltpu.SemaphoreType.DMA],
        compiler_params=pltpu.CompilerParams(vmem_limit_bytes=VMEM_LIMIT),
        name=f"leave_{group}",
    )(meta, *parts, *([] if out is None else [out]))


def local(raw_stack, psf_taps):
    me = lax.axis_index("gx") * 8 + lax.axis_index("gy")
    channel = lax.rem(lax.axis_index("gy"), 2)
    meta = lax.dynamic_index_in_dim(jnp.asarray(meta_table()), me, keepdims=False)
    taps = lax.dynamic_index_in_dim(psf_taps, channel, axis=1, keepdims=False)
    taps = taps / jnp.sum(taps, axis=1, keepdims=True)

    blocks = destripe(raw_stack).reshape(128, 64, 128)
    got = lax.all_to_all(blocks, AXES, split_axis=0, concat_axis=0, tiled=True)
    tables = filter_tables(taps)
    cleaned, halves, halos = [None, None], [None, None], [None, None]

    def exchange(side):
        halos[1 - side] = lax.ppermute(halves[side][0], AXES, DOWN if side == 0 else UP)

    first = 0
    for side in (first, 1 - first):
        cleaned[side], *halves[side] = arrive(side, got, tables[0])
        exchange(side)

    estimate = list(cleaned)
    for blur in range(2 * ITERS):
        way = blur % 2
        first = 1 - first
        partials = [None, None]
        for side in (first, 1 - first):
            partials[side] = own_lines(way, side, taps, halves)
        if blur == 2 * ITERS - 1:
            break
        arrived = list(halos)
        halves = [None, None]
        for side in (first, 1 - first):
            args = (side, taps, meta, partials[side], arrived[side])
            if way == 0:
                halves[side] = step(True, *args, cleaned[side], tables[1])
            else:
                estimate[side], *halves[side] = step(False, *args, estimate[side], tables[0])
            exchange(side)
    parts = []
    for j in range(ROUNDS):
        part = last(j, taps, meta, partials, halos, estimate)
        parts.append(lax.ppermute(part, AXES, FINAL[j]))
    out = leave(0, meta, parts[:4])
    out = leave(1, meta, parts[4:], out)
    return out.reshape(CH, NZ, 32, 128)


def solution(mesh):
    in_specs = (P(None, AXES, None, None), P())
    out_specs = P(None, None, "gy", "gx")
    return jax.shard_map(local, mesh=mesh, in_specs=in_specs, out_specs=out_specs, check_vma=False)
```
